512 devices in a mesh: grp: 16 (over z_lo, x), fsdp: 4 (over y), tp: 8 (over z_hi, core).
Axes of the slice: x: 4, y: 4, z: 16 (z_hi: 4, z_lo: 4; z = z_hi * 4 + z_lo), core: 2. Of those that a mesh axis runs over, the one named last changes fastest.
Arguments:
- frames: bfloat16 [3072, 5120], P('fsdp', 'grp'), may hold values from -6 to 6
- projector: bfloat16 [5120, 8192], P('grp', 'tp'), may hold values from -0.078125 to 0.078125
- text_token_embedding: bfloat16 [16384, 8192], P(('grp', 'fsdp'), 'tp'), may hold values from -6 to 6
- norm_gain_vector: float32 [8192], replicated, may hold values from 0.1 to 1.9
- frozen: bfloat16 [8192, 1024], P('fsdp', 'tp'), may hold values from -0.0625 to 0.0625
- adapter_down_map: bfloat16 [8192, 64], P('fsdp'), may hold values from -0.0625 to 0.0625
- adapter_up_map: bfloat16 [64, 1024], P(None, 'tp'), may hold values from -0.75 to 0.75
- clip_frame_length: int32 [4, 16, 16], P('fsdp'), may hold values from 1 to 6, as said below
- audio_first_token: int32 [4, 16, 16], P('fsdp'), may hold values from 0 to 255, as said below
- segment_document_index: int32 [16384], P(('grp', 'fsdp')), may hold values from 0 to 255, never falling along the last dimension, each value on 1 to 256 neighbouring positions
- keep_document_flags: int32 [256], replicated, may hold values 0 or 1
- cotangent: bfloat16 [16384, 1024], P(('grp', 'fsdp'), 'tp'), may hold values from -0.046875 to 0.046875
Outputs:
- value_output: bfloat16 [16384, 1024], P(('grp', 'fsdp'), 'tp')
- projector_grad: float32 [5120, 8192], P('grp', 'tp')
- down_map_gradient: float32 [8192, 64], P('tp')
- up_map_gradient: float32 [64, 1024], P(None, 'tp')
The draws below stay inside these ranges and needn't reach their ends.
Inputs may be any that keep to these rules, and one draw needn't show every extreme that they name: `clip_frame_length`: entry [f, g, k] is the length of clip k of frame block f * 16 + g; the 16 clips of a block sum to 48, and one of them has exactly 6 frames. `audio_first_token`: entry [f, g, k] is the first token, among the 256 tokens of block k * 4 + f, of the audio slots of clip k of frame block f * 16 + g; the 16 clips that one token block takes lie in distinct aligned windows of 16 tokens.
All inputs are finite; a program needn't handle non-finite values.
Results may differ from the reference program's by a relative error of at most 0.018.
Values may be sent and summed in bfloat16 or wider, within the bound.
No kernel may reach another device: no remote copies, remote signals or barrier semaphores. Data moves between devices by JAX's collectives and lax.ppermute only.
A program may use at most 128 MiB of HBM per device.

```python
import math
import jax
import jax.numpy as jnp
import numpy as np
from jax import lax

MODEL_WIDTH = 8192
VALUE_WIDTH = 1024
DA = 5120
ADAPTER_RANK = 64
TOK_DEV = 256
FRAMES_DEV = 48
CAP = 6
WIN = 16
TOKENS = 16384
FRAMES = 3072
DOCS = 256
N_GRP = 16
N_FSDP = 4
N_TP = 8


def clip_layout(key):
    base_key = jax.random.fold_in(key, 7321)
    key_order, key_shift, key_window, key_offset = jax.random.split(base_key, 4)
    rows_total = N_FSDP * N_GRP
    half_cap = CAP // 2
    pair_count = (N_GRP - 3) // 2
    scores = jax.random.randint(key_order, (rows_total, N_GRP), 0, 1 << 20) * N_GRP + lax.broadcasted_iota(jnp.int32, (rows_total, N_GRP), 1)
    ranking = jnp.argsort(scores, axis=1, stable=True).astype(jnp.int32)
    deltas = jax.random.randint(key_shift, (rows_total, pair_count), -(half_cap - 1), half_cap)
    adjust = jnp.zeros((rows_total, N_GRP), jnp.int32)
    adjust = adjust.at[:, 0].set(half_cap)
    adjust = adjust.at[:, 1].set(-(half_cap // 2))
    adjust = adjust.at[:, 2].set(-(half_cap - half_cap // 2))
    adjust = adjust.at[:, 3:3 + 2 * pair_count:2].set(deltas)
    adjust = adjust.at[:, 4:4 + 2 * pair_count:2].set(-deltas)
    by_rank = half_cap + adjust
    inverse = jnp.argsort(ranking, axis=1, stable=True).astype(jnp.int32)
    clip_sizes = jnp.take_along_axis(by_rank, inverse, axis=1).reshape(N_FSDP, N_GRP, N_GRP)
    window_scores = jax.random.randint(key_window, (N_FSDP, N_GRP, N_GRP), 0, 1 << 20) * N_GRP + lax.broadcasted_iota(jnp.int32, (N_FSDP, N_GRP, N_GRP), 1)
    window = jnp.argsort(window_scores, axis=1, stable=True).astype(jnp.int32)
    free_room = WIN - clip_sizes + 1
    offsets = jax.random.randint(key_offset, (N_FSDP, N_GRP, N_GRP), 0, free_room)
    positions = window * WIN + offsets
    return (clip_sizes.astype(jnp.int32), positions.astype(jnp.int32))


def draw_clip_frame_length(key, part):
    return clip_layout(key)[0]


def draw_audio_first_token(key, part):
    return clip_layout(key)[1]


def touch_ends(values, key, smallest, largest):
    longest = values.shape.index(max(values.shape))
    spots = []
    for shift in (0, 1):
        where = [jax.random.randint(jax.random.fold_in(key, axis), (), 0, length) for axis, length in enumerate(values.shape)]
        where[longest] = (where[longest] + shift) % values.shape[longest]
        spots.append(tuple(where))
    return values.at[spots[0]].set(smallest).at[spots[1]].set(largest)


def block_scale(rng, dims, cuts, low, high):
    level = 1.0
    for dim, parts in cuts:
        heights = jax.random.uniform(jax.random.fold_in(jax.random.fold_in(rng, 6), dim), (parts,), jnp.float32, low / len(cuts), high / len(cuts))
        level = level * jnp.repeat(jnp.exp(heights), dims[dim] // parts).reshape((-1,) + (1,) * (len(dims) - 1 - dim))
    return level


def length_profile(amount, total, limit, lean):
    weights = [(1 << 20) // math.isqrt(rank ** lean) + 1 for rank in range(2, amount + 1)]
    spare, counts = total - limit - (amount - 1), [1] * (amount - 1)
    while spare > 0:
        free = [i for i in range(amount - 1) if counts[i] < limit]
        whole, remaining = sum([weights[i] for i in free]), spare
        for i in free:
            more = min(limit - counts[i], max(1, remaining * weights[i] // whole), spare)
            counts[i] = counts[i] + more
            spare = spare - more
    return np.array([limit] + counts)


def uneven(rng, count, total, bound, skew):
    if count == 2:
        one = jax.random.randint(rng, (), max(1, total - bound), min(bound, total - 1) + 1)
        return jnp.stack([one, total - one])
    tallies = jnp.asarray(length_profile(count, total, bound, skew), jnp.int32)
    twos = (count - 1) // 2
    giver, taker = tallies[1:1 + 2 * twos:2], tallies[2:2 + 2 * twos:2]
    room = jnp.minimum(giver - 1, bound - taker)
    moved = jax.random.randint(jax.random.fold_in(rng, 1), (twos,), 0, 1 << 20) % (room + 1)
    tallies = tallies.at[1:1 + 2 * twos:2].set(giver - moved).at[2:2 + 2 * twos:2].set(taker + moved)
    return tallies[jax.random.permutation(jax.random.fold_in(rng, 2), count)]


def gaussian(stream_key, dims, scale, limit, shards=(), held_as=jnp.bfloat16):
    entries = scale * jax.random.normal(stream_key, dims, jnp.float32)
    if shards:
        entries = entries * block_scale(stream_key, dims, shards, -0.22, 0.18)
    return jnp.clip(entries, -limit, limit).astype(held_as)


def setup_inputs(seed: int = 0) -> dict:
    keys = jax.random.split(jax.random.key(seed), 13)
    frames = gaussian(keys[0], (FRAMES, DA), 1.0, 6.0, ((0, 4), (1, 16)))
    projector = gaussian(keys[1], (DA, MODEL_WIDTH), DA ** -0.5, 0.078125, ((0, 16), (1, 8)))
    text_token_embedding = gaussian(keys[2], (TOKENS, MODEL_WIDTH), 1.0, 6.0, ((0, 64), (1, 8)))
    norm_gain_vector = jnp.clip(1.0 + 0.18 * jax.random.normal(keys[3], (MODEL_WIDTH,), jnp.float32), 0.1, 1.9)
    frozen = gaussian(keys[4], (MODEL_WIDTH, VALUE_WIDTH), MODEL_WIDTH ** -0.5, 0.0625, ((0, 4), (1, 8)))
    adapter_down_map = gaussian(keys[5], (MODEL_WIDTH, ADAPTER_RANK), MODEL_WIDTH ** -0.5, 0.0625, ((0, 4),))
    adapter_up_map = gaussian(keys[6], (ADAPTER_RANK, VALUE_WIDTH), ADAPTER_RANK ** -0.5, 0.75, ((1, 8),))
    clip_frame_length = draw_clip_frame_length(jax.random.fold_in(keys[12], 71), 0)
    audio_first_token = draw_audio_first_token(jax.random.fold_in(keys[12], 71), 0)
    segment_document_index = jnp.searchsorted(jnp.cumsum(uneven(keys[9], DOCS, TOKENS, 256, 1)), jnp.arange(TOKENS), side="right").astype(jnp.int32)
    keep_document_flags = touch_ends((jax.random.randint(keys[10], (DOCS,), 0, 4) < 3).astype(jnp.int32), jax.random.fold_in(keys[10], 1), 0, 1)
    cotangent = gaussian(keys[11], (TOKENS, VALUE_WIDTH), TOKENS ** -0.5, 0.046875, ((0, 64), (1, 8)))
    return dict(frames=frames, projector=projector, text_token_embedding=text_token_embedding, norm_gain_vector=norm_gain_vector, frozen=frozen, adapter_down_map=adapter_down_map, adapter_up_map=adapter_up_map, clip_frame_length=clip_frame_length, audio_first_token=audio_first_token, segment_document_index=segment_document_index, keep_document_flags=keep_document_flags, cotangent=cotangent)


adapter_scale = 2.0
norm_eps = 1e-05

def reference(frames, projector, text_token_embedding, norm_gain_vector, frozen, adapter_down_map, adapter_up_map, clip_frame_length, audio_first_token, segment_document_index, keep_document_flags, cotangent):
    feat_block = DA // N_GRP
    embed_sum = jnp.zeros((FRAMES, MODEL_WIDTH), jnp.float32)
    for block_id in range(N_GRP):
        low_edge = block_id * feat_block
        partial_sum = jnp.dot(frames[:, low_edge:low_edge + feat_block], projector[low_edge:low_edge + feat_block], preferred_element_type=jnp.float32).astype(jnp.bfloat16)
        partial_sum = lax.optimization_barrier(partial_sum)
        embed_sum = embed_sum + partial_sum.astype(jnp.float32)
    embedded = embed_sum.astype(jnp.bfloat16)
    starts_grid = jnp.cumsum(clip_frame_length, axis=2) - clip_frame_length
    ends_grid = jnp.cumsum(clip_frame_length, axis=2)
    frame_local = lax.broadcasted_iota(jnp.int32, (N_FSDP, N_GRP, FRAMES_DEV), 2)
    clip_index = lax.optimization_barrier(jnp.sum((ends_grid[:, :, None, :] <= frame_local[:, :, :, None]).astype(jnp.int32), axis=3))
    onehot = clip_index[:, :, :, None] == lax.broadcasted_iota(jnp.int32, (1, 1, 1, N_GRP), 3)
    clip_start = lax.optimization_barrier(jnp.sum(jnp.where(onehot, starts_grid[:, :, None, :], 0), axis=3))
    token_start = lax.optimization_barrier(jnp.sum(jnp.where(onehot, audio_first_token[:, :, None, :], 0), axis=3))
    fsdp_iota = lax.broadcasted_iota(jnp.int32, (N_FSDP, N_GRP, FRAMES_DEV), 0)
    token_index = (clip_index * N_FSDP + fsdp_iota) * TOK_DEV + token_start + frame_local - clip_start
    token_flattened = token_index.reshape(FRAMES).astype(jnp.int32)
    inputs = text_token_embedding.at[token_flattened].set(embedded)
    widened = inputs.astype(jnp.float32)
    mean_sq = lax.optimization_barrier(jnp.mean(widened * widened, axis=1))
    inv_rms = lax.rsqrt(mean_sq + norm_eps)
    normalized_input = (widened * inv_rms[:, None] * norm_gain_vector[None, :]).astype(jnp.bfloat16)
    base_output = jnp.dot(normalized_input, frozen, preferred_element_type=jnp.float32)
    lower_rank_rows = jnp.dot(normalized_input, adapter_down_map, preferred_element_type=jnp.float32)
    lower_halfway = lower_rank_rows.astype(jnp.bfloat16)
    value_output = (base_output + adapter_scale * jnp.dot(lower_halfway, adapter_up_map, preferred_element_type=jnp.float32)).astype(jnp.bfloat16)
    weight_tok = keep_document_flags[segment_document_index]
    output_gradient = cotangent * weight_tok.astype(jnp.bfloat16)[:, None]
    up_map_gradient = adapter_scale * jnp.dot(lower_halfway.T, output_gradient, preferred_element_type=jnp.float32)
    adapter_gradient = adapter_scale * jnp.dot(output_gradient, adapter_up_map.T, preferred_element_type=jnp.float32)
    adapter_halfway = adapter_gradient.astype(jnp.bfloat16)
    row_dot_products = lax.optimization_barrier(jnp.sum(output_gradient.astype(jnp.float32) * base_output, axis=1)) + lax.optimization_barrier(jnp.sum(adapter_gradient * lower_rank_rows, axis=1))
    down_map_gradient = jnp.dot(normalized_input.T, adapter_halfway, preferred_element_type=jnp.float32)
    audio_grad = output_gradient[token_flattened]
    tp_cols = VALUE_WIDTH // N_TP
    spread_rows = jnp.zeros((FRAMES, MODEL_WIDTH), jnp.float32)
    for block_id in range(N_TP):
        low_edge = block_id * tp_cols
        partial_sum = jnp.dot(audio_grad[:, low_edge:low_edge + tp_cols], frozen[:, low_edge:low_edge + tp_cols].T, preferred_element_type=jnp.float32).astype(jnp.bfloat16)
        partial_sum = lax.optimization_barrier(partial_sum)
        spread_rows = spread_rows + partial_sum.astype(jnp.float32)
    gradient_norm = spread_rows + jnp.dot(adapter_halfway[token_flattened], adapter_down_map.T, preferred_element_type=jnp.float32)
    audio_inv = inv_rms[token_flattened]
    audio_dot = row_dot_products[token_flattened]
    frame_grad = (audio_inv[:, None] * norm_gain_vector[None, :] * gradient_norm - embedded.astype(jnp.float32) * (audio_inv * audio_inv * audio_dot / MODEL_WIDTH)[:, None]).astype(jnp.bfloat16)
    projector_grad = jnp.dot(frames.T, frame_grad, preferred_element_type=jnp.float32)
    return (value_output, projector_grad, down_map_gradient, up_map_gradient)
```

```python
import jax
import jax.numpy as jnp
from jax import lax
from jax.sharding import Mesh, PartitionSpec as P

adapter_scale = 2.0
norm_eps = 1e-05
GRP = ("zl", "x")
TP = ("zh", "c")
bf16, f32 = jnp.bfloat16, jnp.float32


def dot(a, b, ca, cb):
    return lax.dot_general(a, b, (((ca,), (cb,)), ((), ())), preferred_element_type=f32)


def exchange(blocks, axis):
    return lax.all_to_all(blocks, axis, split_axis=0, concat_axis=0, tiled=True)


def pick_entry(grid_in, position, which_axis):
    matches = lax.broadcasted_iota(jnp.int32, grid_in.shape, which_axis) == position
    return jnp.sum(jnp.where(matches, grid_in, 0), axis=which_axis)


def copies(x, n):
    return jnp.broadcast_to(x[None], (n, *x.shape))


def two_halves(v):
    hi = lax.reduce_precision(v, 8, 7)
    return hi.astype(bf16), (v - hi).astype(bf16)


def shards(
    frames,
    projector,
    text,
    gain_all,
    frozen,
    down,
    up,
    clip_len,
    first_token,
    segment,
    keep,
    cotangent,
):
    nx, ny, ng, nt = (lax.axis_size(a) for a in ("x", "y", GRP, TP))
    grp_index, tp_index = lax.axis_index(GRP), lax.axis_index(TP)
    x_index = lax.axis_index("x")
    toks, width = text.shape
    cols, rank = frozen.shape[1], down.shape[1]
    n_frames = frames.shape[0] // ng
    full_width = width * nt
    cap = 2 * n_frames // ng
    slots = ng * cap
    rows = toks + n_frames
    gain = lax.dynamic_slice_in_dim(gain_all, tp_index * width, width, 0)

    partial = dot(frames, projector, 1, 0).astype(bf16)

    own_sizes = pick_entry(clip_len[0], grp_index, 0)
    before = lax.broadcasted_iota(jnp.int32, (ng, ng), 1) < lax.broadcasted_iota(jnp.int32, (ng, ng), 0)
    own_starts = jnp.sum(jnp.where(before, own_sizes[None, :], 0), axis=1)
    slot_offset = lax.broadcasted_iota(jnp.int32, (ng, cap), 1)
    frame_slot = own_starts[:, None] + slot_offset
    slot_live = slot_offset < own_sizes[:, None]
    frame_iota = lax.broadcasted_iota(jnp.int32, (ng, cap, n_frames), 2)
    sender = (
        ((frame_iota == frame_slot[:, :, None]) & slot_live[:, :, None])
        .astype(bf16)
        .reshape(slots, n_frames)
    )
    in_sizes = pick_entry(clip_len[0], grp_index, 1)
    arrive_at = pick_entry(first_token[0], grp_index, 1)
    token_iota = lax.broadcasted_iota(jnp.int32, (toks, ng, cap), 0)
    receive_mask = (token_iota == (arrive_at[:, None] + slot_offset)[None]) & (
        slot_offset < in_sizes[:, None]
    )[None]
    receiver = receive_mask.astype(bf16).reshape(toks, slots)
    is_audio = jnp.any(receive_mask, axis=(1, 2))

    doc_iota = lax.broadcasted_iota(jnp.int32, (toks, keep.shape[0]), 1)
    kept = jnp.sum(jnp.where(segment[:, None] == doc_iota, keep[None, :], 0), axis=1)
    grad_tok = cotangent * kept.astype(bf16)[:, None]
    grad_slots = exchange(dot(receiver, grad_tok, 0, 0).astype(bf16).reshape(ng, cap, cols), GRP)
    grad_frames = dot(sender, grad_slots.reshape(slots, cols), 0, 0).astype(bf16)
    grad_text = jnp.where(is_audio[:, None], jnp.zeros_like(grad_tok), grad_tok)
    grad_rows = jnp.concatenate([grad_text, grad_frames], axis=0)

    piece = width // (ny * nx)
    w_piece = lax.dynamic_index_in_dim(frozen.reshape(2, ny, nx, piece, cols), x_index, 2, False)
    a_rows = piece // nt
    a_piece = lax.dynamic_index_in_dim(down.reshape(2, ny, nx, nt, a_rows, rank), x_index, 2, False)
    a_piece = lax.dynamic_index_in_dim(a_piece, tp_index, 2, False)
    a_piece = jnp.pad(a_piece, ((0, 0), (0, 0), (0, 0), (0, cols - rank)))
    wa = jnp.moveaxis(jnp.concatenate([w_piece, a_piece], axis=2), 0, 1)
    wa = exchange(wa.reshape(ny, 2 * (piece + a_rows), cols), "y")
    wa = wa.reshape(nt, piece + a_rows, cols)
    lanes = -(-rows // cols) * cols
    padded_grad = jnp.pad(grad_rows, ((0, lanes - rows), (0, 0)))
    lora_part = (adapter_scale * dot(up, padded_grad, 1, 1)).astype(bf16)
    n_l = lanes // cols
    lora_part = jnp.moveaxis(lora_part.reshape(rank, n_l, cols), 1, 0).reshape(n_l * rank, cols)
    sent = jnp.concatenate([wa, copies(jnp.concatenate([grad_frames, lora_part], axis=0), nt)], axis=1)
    came = exchange(sent, TP)
    at = piece + a_rows
    w_rows = jnp.moveaxis(came[:, :piece], 0, 1).reshape(piece, nt * cols)
    weights = jnp.concatenate([w_rows, came[:, piece:at].reshape(piece, cols)], axis=1)
    weights = lax.all_gather(weights, "x", axis=0, tiled=True)
    weights = lax.all_gather(weights, "y", axis=0, tiled=True)
    grad_full = jnp.moveaxis(came[:, at : at + n_frames], 0, 1).reshape(n_frames, nt * cols)
    lora = jnp.sum(came[:, at + n_frames :].astype(f32), axis=0).astype(bf16)
    lora_t = jnp.moveaxis(lora.reshape(n_l, rank, cols), 0, 1).reshape(rank, lanes)[:, :rows]

    blocks = exchange(partial.reshape(ng, n_frames, width), GRP)
    embedded = jnp.sum(blocks.astype(f32), axis=0).astype(bf16)
    inputs = jnp.concatenate([text, embedded], axis=0)
    wide = inputs.astype(f32)
    scaled = wide * gain[None, :]
    sq_part = jnp.sum(wide * wide, axis=1)

    lora_frames = jnp.pad(lora_t[:, toks:].T, ((0, 0), (0, cols - rank)))
    grad_norm = dot(jnp.concatenate([grad_full, lora_frames], axis=1), weights, 1, 1)
    dots_part = jnp.sum(scaled[toks:] * grad_norm, axis=1)
    product = dot(scaled.astype(bf16), weights, 1, 0)
    low_part = product[:, nt * cols : nt * cols + rank].astype(bf16)
    low_part = jnp.pad(low_part.T, ((0, 0), (0, lanes - rows)))
    low_part = jnp.moveaxis(low_part.reshape(rank, n_l, cols), 1, 0).reshape(n_l * rank, cols)
    sums = jnp.pad(jnp.concatenate([sq_part, dots_part]), (0, lanes - rows - n_frames))
    hi, lo = two_halves(sums.reshape(n_l, cols))
    stats = jnp.concatenate([low_part, hi, lo, jnp.zeros((8 - 2 * n_l, cols), bf16)], axis=0)
    stats = jnp.sum(exchange(copies(stats, nt), TP).astype(f32), axis=0)
    sums = (stats[n_l * rank : n_l * rank + n_l] + stats[n_l * rank + n_l : n_l * rank + 2 * n_l]).reshape(lanes)
    inv_rms = lax.rsqrt(sums[:rows] / full_width + norm_eps)
    low = jnp.moveaxis(stats[: n_l * rank].reshape(n_l, rank, cols), 0, 1).reshape(rank, lanes)[:, :rows]
    low_half_t = (low * inv_rms[None, :]).astype(bf16)

    base = jnp.moveaxis(product[:, : nt * cols].astype(bf16).reshape(rows, nt, cols), 1, 0)
    base = lax.psum_scatter(base.reshape(nt * rows, cols), TP, scatter_dimension=0, tiled=True)
    values = base.astype(f32) * inv_rms[:, None] + adapter_scale * dot(low_half_t, up, 0, 0)
    values = values.astype(bf16)

    normed = (scaled * inv_rms[:, None]).astype(bf16)
    down_t = dot(lora_t, normed, 1, 0)
    up_part = adapter_scale * dot(low_half_t, grad_rows, 1, 0)
    adapters = jnp.concatenate(
        [
            down_t.astype(bf16).reshape(ng, rank // ng, width),
            jnp.pad(up_part.astype(bf16), ((0, 0), (0, width - cols))).reshape(ng, rank // ng, width),
        ],
        axis=1,
    )

    inv_f = inv_rms[toks:, None]
    dots = inv_f * sums[rows : rows + n_frames, None]
    frame_grad = (inv_f * gain[None, :] * grad_norm - wide[toks:] * (inv_f * inv_f * dots / full_width)).astype(bf16)
    came = exchange(jnp.concatenate([copies(frame_grad, ng), adapters], axis=1), GRP)
    all_grad = came[:, :n_frames].reshape(ng * n_frames, width)
    adapters = jnp.sum(came[:, n_frames:].astype(f32), axis=0).astype(bf16)
    proj_part = dot(frames, all_grad, 0, 0).astype(bf16)
    third = frames.shape[1] // ny
    came = exchange(
        jnp.concatenate([proj_part.reshape(ny, third, width), copies(adapters, ny)], axis=1), "y"
    )
    came = jnp.sum(came.astype(f32), axis=0)
    projector_grad = lax.all_gather(came[:third].astype(bf16), "y", axis=0, tiled=True).astype(f32)

    k = rank // ng
    own = jnp.concatenate([came[third : third + k].reshape(k * width // cols, cols), came[third + k :, :cols]], axis=0)
    out_slots = dot(sender, values[toks:], 1, 0).reshape(ng, cap, cols)
    last = exchange(jnp.concatenate([copies(own, ng), out_slots], axis=1), GRP)
    n_d = k * width // cols
    down_grad = last[:, :n_d].reshape(rank, width).T
    up_grad = last[:, n_d : n_d + k].reshape(rank, cols)
    in_slots = last[:, n_d + k :].astype(bf16).reshape(slots, cols)
    audio_values = dot(receiver, in_slots, 1, 0).astype(bf16)
    value_output = jnp.where(is_audio[:, None], audio_values, values[:toks])
    return value_output, projector_grad, down_grad, up_grad


def solution(mesh):
    sizes = dict(zip(mesh.axis_names, mesh.devices.shape))
    half = sizes["grp"] // 4
    mesh = Mesh(
        mesh.devices.reshape(half, 4, sizes["fsdp"], sizes["tp"] // 2, 2),
        ("zl", "x", "y", "zh", "c"),
    )
    rows = ("zl", "x", "y")
    in_specs = (
        P("y", GRP),
        P(GRP, TP),
        P(rows, TP),
        P(),
        P("y", TP),
        P("y", None),
        P(None, TP),
        P("y", None, None),
        P("y", None, None),
        P(rows),
        P(),
        P(rows, TP),
    )
    out_specs = (P(rows, TP), P(GRP, TP), P(TP, None), P(None, TP))
    return jax.shard_map(shards, mesh=mesh, in_specs=in_specs, out_specs=out_specs, check_vma=False)
```

```python
import jax
import jax.numpy as jnp
from jax import lax
from jax.sharding import Mesh, PartitionSpec as P

adapter_scale = 2.0
norm_eps = 1e-05
GRP = ("zl", "x")
TP = ("zh", "c")
bf16, f32 = jnp.bfloat16, jnp.float32


def dot(a, b, ca, cb):
    return lax.dot_general(a, b, (((ca,), (cb,)), ((), ())), preferred_element_type=f32)


def exchange(blocks, axis):
    return lax.all_to_all(blocks, axis, split_axis=0, concat_axis=0, tiled=True)


def pick_entry(grid_in, position, which_axis):
    matches = lax.broadcasted_iota(jnp.int32, grid_in.shape, which_axis) == position
    return jnp.sum(jnp.where(matches, grid_in, 0), axis=which_axis)


def copies(x, n):
    return jnp.broadcast_to(x[None], (n, *x.shape))


def two_halves(v):
    hi = lax.reduce_precision(v, 8, 7)
    return hi.astype(bf16), (v - hi).astype(bf16)


def from_peers(x, axis):
    n = lax.axis_size(axis)
    return [x] + [lax.ppermute(x, axis, [(i, (i + k) % n) for i in range(n)]) for k in range(1, n)]


def placed(blocks, dim, axis):
    n, me, size = len(blocks), lax.axis_index(axis), blocks[0].shape[dim]
    shape = list(blocks[0].shape)
    shape[dim] *= n
    out = jnp.zeros(shape, blocks[0].dtype)
    for k, block in enumerate(blocks):
        out = lax.dynamic_update_slice_in_dim(out, block, lax.rem(me - k + n, n) * size, dim)
    return out


def shards(
    frames,
    projector,
    text,
    gain_all,
    frozen,
    down,
    up,
    clip_len,
    first_token,
    segment,
    keep,
    cotangent,
):
    nx, ny, nzl, ng, nt = (lax.axis_size(a) for a in ("x", "y", "zl", GRP, TP))
    grp_index, tp_index = lax.axis_index(GRP), lax.axis_index(TP)
    x_index, y_index = lax.axis_index("x"), lax.axis_index("y")
    toks, width = text.shape
    cols, rank = frozen.shape[1], down.shape[1]
    n_frames = frames.shape[0] // ng
    full_width = width * nt
    cap = 2 * n_frames // ng
    slots = ng * cap
    rows = toks + n_frames
    gain = lax.dynamic_slice_in_dim(gain_all, tp_index * width, width, 0)

    by_x = frames.reshape(nzl, nx, n_frames, frames.shape[1])

    def block_for(k):
        part = lax.dynamic_index_in_dim(by_x, lax.rem(x_index + k, nx), 1, False)
        part = part.reshape(nzl * n_frames, frames.shape[1])
        return dot(part, projector, 1, 0).astype(bf16)

    x_parts = [
        lax.ppermute(block_for(k), "x", [(i, (i + k) % nx) for i in range(nx)]) for k in range(1, nx)
    ]
    x_sum = block_for(0).astype(f32)
    for part in x_parts:
        x_sum = x_sum + part.astype(f32)

    own_sizes = pick_entry(clip_len[0], grp_index, 0)
    before = lax.broadcasted_iota(jnp.int32, (ng, ng), 1) < lax.broadcasted_iota(jnp.int32, (ng, ng), 0)
    own_starts = jnp.sum(jnp.where(before, own_sizes[None, :], 0), axis=1)
    slot_offset = lax.broadcasted_iota(jnp.int32, (ng, cap), 1)
    frame_slot = own_starts[:, None] + slot_offset
    slot_live = slot_offset < own_sizes[:, None]
    frame_iota = lax.broadcasted_iota(jnp.int32, (ng, cap, n_frames), 2)
    sender = (
        ((frame_iota == frame_slot[:, :, None]) & slot_live[:, :, None])
        .astype(bf16)
        .reshape(slots, n_frames)
    )
    in_sizes = pick_entry(clip_len[0], grp_index, 1)
    arrive_at = pick_entry(first_token[0], grp_index, 1)
    token_iota = lax.broadcasted_iota(jnp.int32, (toks, ng, cap), 0)
    receive_mask = (token_iota == (arrive_at[:, None] + slot_offset)[None]) & (
        slot_offset < in_sizes[:, None]
    )[None]
    receiver = receive_mask.astype(bf16).reshape(toks, slots)
    is_audio = jnp.any(receive_mask, axis=(1, 2))

    doc_iota = lax.broadcasted_iota(jnp.int32, (toks, keep.shape[0]), 1)
    kept = jnp.sum(jnp.where(segment[:, None] == doc_iota, keep[None, :], 0), axis=1)
    grad_tok = cotangent * kept.astype(bf16)[:, None]
    grad_slots = exchange(dot(receiver, grad_tok, 0, 0).astype(bf16).reshape(ng, cap, cols), GRP)
    grad_frames = dot(sender, grad_slots.reshape(slots, cols), 0, 0).astype(bf16)
    grad_text = jnp.where(is_audio[:, None], jnp.zeros_like(grad_tok), grad_tok)
    grad_rows = jnp.concatenate([grad_text, grad_frames], axis=0)

    piece = width // (ny * nx)
    w_piece = lax.dynamic_index_in_dim(frozen.reshape(2, ny, nx, piece, cols), x_index, 2, False)
    down_half = lax.dynamic_slice_in_dim(down.T, lax.rem(tp_index, 2) * width, width, 1)
    down_half = jnp.moveaxis(down_half.reshape(rank, nt, cols), 1, 0).reshape(nt * rank, cols)

    def for_y(k):
        w = lax.dynamic_index_in_dim(w_piece, lax.rem(y_index + k, ny), 1, False)
        return jnp.concatenate([w.reshape(2 * piece, cols), down_half], axis=0)

    y_parts = [for_y(0)] + [
        lax.ppermute(for_y(k), "y", [(i, (i + k) % ny) for i in range(ny)]) for k in range(1, ny)
    ]
    y_parts = jnp.stack([lax.select_n(lax.rem(y_index - j + ny, ny), *y_parts) for j in range(ny)])
    wa = y_parts[:, : 2 * piece].reshape(nt, piece, cols)
    down_t = lax.dynamic_index_in_dim(y_parts[:, 2 * piece :], tp_index // 2, 0, False)
    down_t = jnp.moveaxis(down_t.reshape(nt, rank, cols), 0, 1).reshape(rank, width)
    up_rows = rank // nx
    up_piece = lax.dynamic_slice_in_dim(up, x_index * up_rows, up_rows, 0)
    sent = jnp.concatenate(
        [wa, copies(jnp.concatenate([up_piece, grad_frames], axis=0), nt)], axis=1
    )
    came = exchange(sent, TP)
    at = piece + up_rows
    weights = jnp.moveaxis(came[:, :at], 0, 1).reshape(at, nt * cols)
    weights = lax.all_gather(weights, "x")
    up_full = weights[:, piece:].reshape(rank, nt * cols)
    weights = from_peers(weights[:, :piece].reshape(nx * piece, nt * cols), "y")
    grad_full = jnp.moveaxis(came[:, at:], 0, 1).reshape(n_frames, nt * cols)
    lora_frames = (adapter_scale * dot(grad_full, up_full, 1, 1)).astype(bf16)

    text_wide = text.astype(f32)
    text_scaled = text_wide * gain[None, :]
    pair = jnp.concatenate(
        [
            (adapter_scale * dot(grad_text, up, 1, 1)).astype(bf16),
            dot(text_scaled.astype(bf16), down_t, 1, 1).astype(bf16),
        ],
        axis=1,
    )
    pair = lax.psum_scatter(pair, TP, scatter_dimension=0, tiled=True)
    sq_text = dot(jnp.ones((8, width), bf16), (text_wide * text_wide).astype(bf16), 1, 1)[0]

    blocks = exchange(x_sum.astype(bf16).reshape(nzl, n_frames, width), "zl")
    embedded = jnp.sum(blocks.astype(f32), axis=0).astype(bf16)
    wide = embedded.astype(f32)
    scaled = wide * gain[None, :]

    grad_norm = placed([dot(grad_full, w, 1, 1) for w in weights], 1, "y")
    grad_norm = grad_norm + dot(lora_frames, down_t, 1, 0)
    sq_hi, sq_lo = two_halves(jnp.sum(wide * wide, axis=1, keepdims=True))
    d_hi, d_lo = two_halves(jnp.sum(scaled * grad_norm, axis=1, keepdims=True))
    low_frames = dot(scaled.astype(bf16), down_t, 1, 1).astype(bf16)
    spare = jnp.zeros((n_frames, cols - rank - 4), bf16)
    of_frames = jnp.concatenate([low_frames, sq_hi, sq_lo, d_hi, d_lo, spare], axis=1)
    n_l = toks // cols
    t_hi, t_lo = two_halves(sq_text.reshape(n_l, cols))
    spare = jnp.zeros((8 - 2 * n_l, cols), bf16)
    stats = jnp.concatenate([of_frames, t_hi, t_lo, spare, pair], axis=0)
    stats = exchange(copies(stats, nt), TP)
    pair = stats[:, n_frames + 8 :].reshape(toks, cols)
    stats = jnp.sum(stats[:, : n_frames + 8].astype(f32), axis=0)
    sq_frames = stats[:n_frames, rank : rank + 1] + stats[:n_frames, rank + 1 : rank + 2]
    dots = stats[:n_frames, rank + 2 : rank + 3] + stats[:n_frames, rank + 3 : rank + 4]
    sq_text = (stats[n_frames : n_frames + n_l] + stats[n_frames + n_l : n_frames + 2 * n_l]).reshape(toks, 1)
    inv_text = lax.rsqrt(sq_text / full_width + norm_eps)
    inv_f = lax.rsqrt(sq_frames / full_width + norm_eps)
    inv_rms = jnp.concatenate([inv_text, inv_f], axis=0)
    lora = jnp.concatenate([pair[:, :rank], lora_frames], axis=0)
    low = jnp.concatenate([pair[:, rank:].astype(f32), stats[:n_frames, :rank]], axis=0)
    low_half = (low * inv_rms).astype(bf16)

    all_scaled = jnp.concatenate([text_scaled, scaled], axis=0)
    quarter = width // ny
    base = jnp.zeros((rows, nt * cols), f32)
    for j, w in enumerate(weights):
        at = lax.rem(y_index - j + ny, ny) * quarter
        base = base + dot(lax.dynamic_slice_in_dim(all_scaled, at, quarter, 1).astype(bf16), w, 1, 0)
    base = base.astype(bf16)
    base = jnp.moveaxis(base.reshape(rows, nt, cols), 1, 0)
    base = lax.psum_scatter(base.reshape(nt * rows, cols), TP, scatter_dimension=0, tiled=True)
    values = base.astype(f32) * inv_rms + adapter_scale * dot(low_half, up, 1, 0)
    values = values.astype(bf16)

    normed = (all_scaled * inv_rms).astype(bf16)
    k = rank // ng
    down_part = dot(lora, normed, 0, 0).astype(bf16).reshape(nzl, nx, k, width)
    up_part = (adapter_scale * dot(low_half, grad_rows, 0, 0)).astype(bf16)
    up_part = jnp.pad(up_part, ((0, 0), (0, width - cols))).reshape(nzl, nx, k, width)
    adapters = jnp.concatenate([down_part, up_part], axis=2).reshape(nzl, nx * 2 * k, width)

    frame_grad = (
        inv_f * gain[None, :] * grad_norm - wide * (inv_f * inv_f * inv_f * dots / full_width)
    ).astype(bf16)
    came = exchange(jnp.concatenate([copies(frame_grad, nzl), adapters], axis=1), "zl")
    adapters = jnp.sum(came[:, n_frames:].astype(f32), axis=0).astype(bf16).reshape(nx, 2 * k, width)
    frame_grad = came[:, :n_frames].reshape(nzl * n_frames, width)
    came = exchange(jnp.concatenate([copies(frame_grad, nx), adapters], axis=1), "x")
    adapters = jnp.sum(came[:, nzl * n_frames :].astype(f32), axis=0).astype(bf16)
    all_grad = came[:, : nzl * n_frames].reshape(nx, nzl, n_frames, width)
    all_grad = jnp.moveaxis(all_grad, 0, 1).reshape(ng * n_frames, width)
    proj_part = dot(frames, all_grad, 0, 0).astype(bf16)
    part = frames.shape[1] // ny
    came = exchange(
        jnp.concatenate([proj_part.reshape(ny, part, width), copies(adapters, ny)], axis=1), "y"
    )
    came = jnp.sum(came.astype(f32), axis=0)
    projector_grad = placed([b.astype(f32) for b in from_peers(came[:part].astype(bf16), "y")], 0, "y")

    n_d = k * width // cols
    own = jnp.concatenate([came[part : part + k].reshape(n_d, cols), came[part + k :, :cols]], axis=0)
    out_slots = dot(sender, values[toks:], 1, 0).reshape(ng, cap, cols)
    last = exchange(jnp.concatenate([copies(own, ng), out_slots], axis=1), GRP)
    down_grad = last[:, :n_d].reshape(rank, width).T
    up_grad = last[:, n_d : n_d + k].reshape(rank, cols)
    in_slots = last[:, n_d + k :].astype(bf16).reshape(slots, cols)
    audio_values = dot(receiver, in_slots, 1, 0).astype(bf16)
    value_output = jnp.where(is_audio[:, None], audio_values, values[:toks])
    return value_output, projector_grad, down_grad, up_grad


def solution(mesh):
    sizes = dict(zip(mesh.axis_names, mesh.devices.shape))
    half = sizes["grp"] // 4
    mesh = Mesh(
        mesh.devices.reshape(half, 4, sizes["fsdp"], sizes["tp"] // 2, 2),
        ("zl", "x", "y", "zh", "c"),
    )
    rows = ("zl", "x", "y")
    in_specs = (
        P("y", GRP),
        P(GRP, TP),
        P(rows, TP),
        P(),
        P("y", TP),
        P("y", None),
        P(None, TP),
        P("y", None, None),
        P("y", None, None),
        P(rows),
        P(),
        P(rows, TP),
    )
    out_specs = (P(rows, TP), P(GRP, TP), P(TP, None), P(None, TP))
    return jax.shard_map(shards, mesh=mesh, in_specs=in_specs, out_specs=out_specs, check_vma=False)
```

```python
import jax
import jax.numpy as jnp
from jax import lax
from jax.sharding import Mesh, PartitionSpec as P

adapter_scale = 2.0
norm_eps = 1e-05
GRP = ("zl", "x")
TP = ("zh", "c")
bf16, f32 = jnp.bfloat16, jnp.float32


def dot(a, b, ca, cb):
    return lax.dot_general(a, b, (((ca,), (cb,)), ((), ())), preferred_element_type=f32)


def exchange(blocks, axis):
    return lax.all_to_all(blocks, axis, split_axis=0, concat_axis=0, tiled=True)


def pick_entry(grid_in, position, which_axis):
    matches = lax.broadcasted_iota(jnp.int32, grid_in.shape, which_axis) == position
    return jnp.sum(jnp.where(matches, grid_in, 0), axis=which_axis)


def after(x, other):
    return x + (other[(0,) * other.ndim] * 0).astype(x.dtype)


def copies(x, n):
    return jnp.broadcast_to(x[None], (n, *x.shape))


def two_halves(v):
    hi = lax.reduce_precision(v, 8, 7)
    return hi.astype(bf16), (v - hi).astype(bf16)


def from_peers(x, axis):
    n = lax.axis_size(axis)
    return [x] + [lax.ppermute(x, axis, [(i, (i + k) % n) for i in range(n)]) for k in range(1, n)]


def to_peers(blocks, axis):
    n, me = lax.axis_size(axis), lax.axis_index(axis)
    return [blocks(me)] + [
        lax.ppermute(blocks(lax.rem(me + k, n)), axis, [(i, (i + k) % n) for i in range(n)])
        for k in range(1, n)
    ]


def placed(blocks, dim, axis):
    n, me, size = len(blocks), lax.axis_index(axis), blocks[0].shape[dim]
    shape = list(blocks[0].shape)
    shape[dim] *= n
    out = jnp.zeros(shape, blocks[0].dtype)
    for k, block in enumerate(blocks):
        out = lax.dynamic_update_slice_in_dim(out, block, lax.rem(me - k + n, n) * size, dim)
    return out


def shards(
    frames,
    projector,
    text,
    gain_all,
    frozen,
    down,
    up,
    clip_len,
    first_token,
    segment,
    keep,
    cotangent,
):
    nx, ny, nzl, ng, nt = (lax.axis_size(a) for a in ("x", "y", "zl", GRP, TP))
    grp_index, tp_index = lax.axis_index(GRP), lax.axis_index(TP)
    x_index, y_index = lax.axis_index("x"), lax.axis_index("y")
    toks, width = text.shape
    cols, rank = frozen.shape[1], down.shape[1]
    n_frames = frames.shape[0] // ng
    full_width = width * nt
    cap = 2 * n_frames // ng
    slots = ng * cap
    rows = toks + n_frames
    gain = lax.dynamic_slice_in_dim(gain_all, tp_index * width, width, 0)

    own_sizes = pick_entry(clip_len[0], grp_index, 0)
    before = lax.broadcasted_iota(jnp.int32, (ng, ng), 1) < lax.broadcasted_iota(jnp.int32, (ng, ng), 0)
    own_starts = jnp.sum(jnp.where(before, own_sizes[None, :], 0), axis=1)
    slot_offset = lax.broadcasted_iota(jnp.int32, (ng, cap), 1)
    frame_slot = own_starts[:, None] + slot_offset
    slot_live = slot_offset < own_sizes[:, None]
    frame_iota = lax.broadcasted_iota(jnp.int32, (ng, cap, n_frames), 2)
    sender = (
        ((frame_iota == frame_slot[:, :, None]) & slot_live[:, :, None])
        .astype(bf16)
        .reshape(slots, n_frames)
    )
    in_sizes = pick_entry(clip_len[0], grp_index, 1)
    arrive_at = pick_entry(first_token[0], grp_index, 1)
    token_iota = lax.broadcasted_iota(jnp.int32, (toks, ng, cap), 0)
    receive_mask = (token_iota == (arrive_at[:, None] + slot_offset)[None]) & (
        slot_offset < in_sizes[:, None]
    )[None]
    receiver = receive_mask.astype(bf16).reshape(toks, slots)
    is_audio = jnp.any(receive_mask, axis=(1, 2))

    doc_iota = lax.broadcasted_iota(jnp.int32, (toks, keep.shape[0]), 1)
    kept = jnp.sum(jnp.where(segment[:, None] == doc_iota, keep[None, :], 0), axis=1)
    grad_tok = cotangent * kept.astype(bf16)[:, None]
    grad_slots = exchange(dot(receiver, grad_tok, 0, 0).astype(bf16).reshape(ng, cap, cols), GRP)
    grad_frames = dot(sender, grad_slots.reshape(slots, cols), 0, 0).astype(bf16)
    grad_text = jnp.where(is_audio[:, None], jnp.zeros_like(grad_tok), grad_tok)
    grad_rows = jnp.concatenate([grad_text, grad_frames], axis=0)

    piece = width // (ny * nx)
    w_piece = lax.dynamic_index_in_dim(frozen.reshape(2, ny, nx, piece, cols), x_index, 2, False)
    down_half = lax.dynamic_slice_in_dim(down.T, lax.rem(tp_index, 2) * width, width, 1)
    down_half = jnp.moveaxis(down_half.reshape(rank, nt, cols), 1, 0).reshape(nt * rank, cols)

    def for_y(k):
        w = lax.dynamic_index_in_dim(w_piece, lax.rem(y_index + k, ny), 1, False)
        return jnp.concatenate([w.reshape(2 * piece, cols), down_half], axis=0)

    y_parts = [for_y(0)] + [
        lax.ppermute(for_y(k), "y", [(i, (i + k) % ny) for i in range(ny)]) for k in range(1, ny)
    ]
    y_parts = jnp.stack([lax.select_n(lax.rem(y_index - j + ny, ny), *y_parts) for j in range(ny)])
    wa = y_parts[:, : 2 * piece].reshape(nt, piece, cols)
    down_t = lax.dynamic_index_in_dim(y_parts[:, 2 * piece :], tp_index // 2, 0, False)
    down_t = jnp.moveaxis(down_t.reshape(nt, rank, cols), 0, 1).reshape(rank, width)
    up_rows = rank // nx
    up_piece = lax.dynamic_slice_in_dim(up, x_index * up_rows, up_rows, 0)
    sent = jnp.concatenate(
        [wa, copies(jnp.concatenate([up_piece, grad_frames], axis=0), nt)], axis=1
    )
    text_wide = text.astype(f32)
    text_scaled = text_wide * gain[None, :]
    pair = jnp.concatenate(
        [
            (adapter_scale * dot(grad_text, up, 1, 1)).astype(bf16),
            dot(text_scaled.astype(bf16), down_t, 1, 1).astype(bf16),
        ],
        axis=1,
    )
    sent, pair, frames_in = lax.optimization_barrier((sent, pair, frames))
    pair = lax.psum_scatter(pair, TP, scatter_dimension=0, tiled=True)
    sq_text = dot(jnp.ones((8, width), bf16), (text_wide * text_wide).astype(bf16), 1, 1)[0]

    came = exchange(sent, TP)

    by_x = frames_in.reshape(nzl, nx, n_frames, frames.shape[1])

    def block_for(k):
        part = lax.dynamic_index_in_dim(by_x, lax.rem(x_index + k, nx), 1, False)
        part = part.reshape(nzl * n_frames, frames.shape[1])
        return dot(part, projector, 1, 0).astype(bf16)

    x_parts = [
        lax.ppermute(block_for(k), "x", [(i, (i + k) % nx) for i in range(nx)]) for k in range(1, nx)
    ]
    x_sum = block_for(0).astype(f32)
    for part in x_parts:
        x_sum = x_sum + part.astype(f32)

    at = piece + up_rows
    grad_full = jnp.moveaxis(came[:, at:], 0, 1).reshape(n_frames, nt * cols)
    grad_all = jnp.concatenate(from_peers(grad_full, "y"), axis=0)
    weights = jnp.moveaxis(came[:, :at], 0, 1).reshape(at, nt * cols)
    weights = lax.all_gather(weights, "x")
    up_full = weights[:, piece:].reshape(rank, nt * cols)
    weights = weights[:, :piece].reshape(nx * piece, nt * cols)
    lora_frames = (adapter_scale * dot(grad_full, up_full, 1, 1)).astype(bf16)
    spread = dot(grad_all, weights, 1, 1).astype(bf16).reshape(ny, n_frames, nx * piece)
    parts = [spread[0]] + [
        lax.ppermute(spread[k], "y", [(i, (i - k) % ny) for i in range(ny)]) for k in range(1, ny)
    ]
    parts = [parts[0]] + parts[:0:-1]
    grad_norm = placed([p.astype(f32) for p in parts], 1, "y")
    grad_norm = grad_norm + dot(lora_frames, down_t, 1, 0)
    weights = lax.all_gather(weights, "y", axis=0, tiled=True)

    blocks = exchange(x_sum.astype(bf16).reshape(nzl, n_frames, width), "zl")
    embedded = jnp.sum(blocks.astype(f32), axis=0).astype(bf16)
    wide = embedded.astype(f32)
    scaled = wide * gain[None, :]

    sq_hi, sq_lo = two_halves(jnp.sum(wide * wide, axis=1, keepdims=True))
    d_hi, d_lo = two_halves(jnp.sum(scaled * grad_norm, axis=1, keepdims=True))
    low_frames = dot(scaled.astype(bf16), down_t, 1, 1).astype(bf16)
    spare = jnp.zeros((n_frames, cols - rank - 4), bf16)
    of_frames = jnp.concatenate([low_frames, sq_hi, sq_lo, d_hi, d_lo, spare], axis=1)
    n_l = toks // cols
    t_hi, t_lo = two_halves(sq_text.reshape(n_l, cols))
    spare = jnp.zeros((8 - 2 * n_l, cols), bf16)
    stats = jnp.concatenate([of_frames, t_hi, t_lo, spare, pair], axis=0)
    stats = exchange(copies(stats, nt), TP)
    pair = stats[:, n_frames + 8 :].reshape(toks, cols)
    stats = jnp.sum(stats[:, : n_frames + 8].astype(f32), axis=0)
    sq_frames = stats[:n_frames, rank : rank + 1] + stats[:n_frames, rank + 1 : rank + 2]
    dots = stats[:n_frames, rank + 2 : rank + 3] + stats[:n_frames, rank + 3 : rank + 4]
    sq_text = (stats[n_frames : n_frames + n_l] + stats[n_frames + n_l : n_frames + 2 * n_l]).reshape(toks, 1)
    inv_rms = lax.rsqrt(jnp.concatenate([sq_text, sq_frames], axis=0) / full_width + norm_eps)
    lora = jnp.concatenate([pair[:, :rank], lora_frames], axis=0)
    low = jnp.concatenate([pair[:, rank:].astype(f32), stats[:n_frames, :rank]], axis=0)
    low_half = (low * inv_rms).astype(bf16)

    all_scaled = jnp.concatenate([text_scaled, scaled], axis=0)
    base = dot(all_scaled.astype(bf16), weights, 1, 0).astype(bf16)
    base = jnp.moveaxis(base.reshape(rows, nt, cols), 1, 0).reshape(nt * rows, cols)
    summed = lax.psum_scatter(base, TP, scatter_dimension=0, tiled=True)
    values = summed.astype(f32) * inv_rms + adapter_scale * dot(low_half, up, 1, 0)
    values = values.astype(bf16)

    normed = (all_scaled * inv_rms).astype(bf16)
    k = rank // ng
    down_part = dot(lora, normed, 0, 0).astype(bf16).reshape(nzl, nx, k, width)
    up_part = (adapter_scale * dot(low_half, grad_rows, 0, 0)).astype(bf16)
    up_part = jnp.pad(up_part, ((0, 0), (0, width - cols))).reshape(nzl, nx, k, width)
    adapters = jnp.concatenate([down_part, up_part], axis=2).reshape(nzl, nx * 2 * k, width)

    inv_f = after(inv_rms[toks:], base)
    frame_grad = (
        inv_f * gain[None, :] * grad_norm - wide * (inv_f * inv_f * inv_f * dots / full_width)
    ).astype(bf16)
    near = to_peers(
        lambda z: jnp.concatenate([frame_grad, lax.dynamic_index_in_dim(adapters, z, 0, False)], axis=0), "zl"
    )
    adapters = sum(b[n_frames:].astype(f32) for b in near).astype(bf16).reshape(nx, 2 * k, width)
    frame_grad = placed([b[:n_frames] for b in near], 0, "zl")
    came = exchange(jnp.concatenate([copies(frame_grad, nx), adapters], axis=1), "x")
    adapters = jnp.sum(came[:, nzl * n_frames :].astype(f32), axis=0).astype(bf16)
    all_grad = came[:, : nzl * n_frames].reshape(nx, nzl, n_frames, width)
    all_grad = jnp.moveaxis(all_grad, 0, 1).reshape(ng * n_frames, width)
    proj_part = dot(frames, all_grad, 0, 0).astype(bf16)
    part = frames.shape[1] // ny
    came = exchange(
        jnp.concatenate([proj_part.reshape(ny, part, width), copies(adapters, ny)], axis=1), "y"
    )
    came = jnp.sum(came.astype(f32), axis=0)
    projector_grad = placed([b.astype(f32) for b in from_peers(came[:part].astype(bf16), "y")], 0, "y")

    n_d = k * width // cols
    own = jnp.concatenate([came[part : part + k].reshape(n_d, cols), came[part + k :, :cols]], axis=0)
    out_slots = dot(sender, values[toks:], 1, 0).reshape(ng, cap, cols)
    last = exchange(jnp.concatenate([copies(own, ng), out_slots], axis=1), GRP)
    down_grad = last[:, :n_d].reshape(rank, width).T
    up_grad = last[:, n_d : n_d + k].reshape(rank, cols)
    in_slots = last[:, n_d + k :].astype(bf16).reshape(slots, cols)
    audio_values = dot(receiver, in_slots, 1, 0).astype(bf16)
    value_output = jnp.where(is_audio[:, None], audio_values, values[:toks])
    return value_output, projector_grad, down_grad, up_grad


def solution(mesh):
    sizes = dict(zip(mesh.axis_names, mesh.devices.shape))
    half = sizes["grp"] // 4
    mesh = Mesh(
        mesh.devices.reshape(half, 4, sizes["fsdp"], sizes["tp"] // 2, 2),
        ("zl", "x", "y", "zh", "c"),
    )
    rows = ("zl", "x", "y")
    in_specs = (
        P("y", GRP),
        P(GRP, TP),
        P(rows, TP),
        P(),
        P("y", TP),
        P("y", None),
        P(None, TP),
        P("y", None, None),
        P("y", None, None),
        P(rows),
        P(),
        P(rows, TP),
    )
    out_specs = (P(rows, TP), P(GRP, TP), P(TP, None), P(None, TP))
    return jax.shard_map(shards, mesh=mesh, in_specs=in_specs, out_specs=out_specs, check_vma=False)
```

```python
import jax
import jax.numpy as jnp
from jax import lax
from jax.sharding import Mesh, PartitionSpec as P

adapter_scale = 2.0
norm_eps = 1e-05
GRP = ("zl", "x")
TP = ("zh", "c")
bf16, f32 = jnp.bfloat16, jnp.float32


def dot(a, b, ca, cb):
    return lax.dot_general(a, b, (((ca,), (cb,)), ((), ())), preferred_element_type=f32)


def exchange(blocks, axis):
    return lax.all_to_all(blocks, axis, split_axis=0, concat_axis=0, tiled=True)


def pick_entry(grid_in, position, which_axis):
    matches = lax.broadcasted_iota(jnp.int32, grid_in.shape, which_axis) == position
    return jnp.sum(jnp.where(matches, grid_in, 0), axis=which_axis)


def after(x, other):
    return x + (other[(0,) * other.ndim] * 0).astype(x.dtype)


def copies(x, n):
    return jnp.broadcast_to(x[None], (n, *x.shape))


def two_halves(v):
    hi = lax.reduce_precision(v, 8, 7)
    return hi.astype(bf16), (v - hi).astype(bf16)


def from_peers(x, axis):
    n = lax.axis_size(axis)
    return [x] + [lax.ppermute(x, axis, [(i, (i + k) % n) for i in range(n)]) for k in range(1, n)]


def in_order(blocks, axis):
    n, me = lax.axis_size(axis), lax.axis_index(axis)
    return jnp.stack([lax.dynamic_index_in_dim(blocks, lax.rem(me - j + n, n), 0, False) for j in range(n)])


def to_peers(blocks, axis):
    n, me = lax.axis_size(axis), lax.axis_index(axis)
    return [blocks(me)] + [
        lax.ppermute(blocks(lax.rem(me + k, n)), axis, [(i, (i + k) % n) for i in range(n)])
        for k in range(1, n)
    ]


def placed(blocks, dim, axis):
    n, me, size = len(blocks), lax.axis_index(axis), blocks[0].shape[dim]
    shape = list(blocks[0].shape)
    shape[dim] *= n
    out = jnp.zeros(shape, blocks[0].dtype)
    for k, block in enumerate(blocks):
        out = lax.dynamic_update_slice_in_dim(out, block, lax.rem(me - k + n, n) * size, dim)
    return out


def shards(
    frames,
    projector,
    text,
    gain_all,
    frozen,
    down,
    up,
    clip_len,
    first_token,
    segment,
    keep,
    cotangent,
):
    nx, ny, nzl, ng, nt = (lax.axis_size(a) for a in ("x", "y", "zl", GRP, TP))
    grp_index, tp_index = lax.axis_index(GRP), lax.axis_index(TP)
    x_index, y_index = lax.axis_index("x"), lax.axis_index("y")
    toks, width = text.shape
    cols, rank = frozen.shape[1], down.shape[1]
    n_frames = frames.shape[0] // ng
    full_width = width * nt
    cap = 2 * n_frames // ng
    slots = ng * cap
    rows = toks + n_frames
    gain = lax.dynamic_slice_in_dim(gain_all, tp_index * width, width, 0)

    by_x = jnp.moveaxis(frames.reshape(nzl, nx, n_frames, frames.shape[1]), 1, 0)
    partial = dot(by_x.reshape(frames.shape), projector, 1, 0).astype(bf16)
    x_sum = lax.psum_scatter(partial, "x", scatter_dimension=0, tiled=True)

    own_sizes = pick_entry(clip_len[0], grp_index, 0)
    before = lax.broadcasted_iota(jnp.int32, (ng, ng), 1) < lax.broadcasted_iota(jnp.int32, (ng, ng), 0)
    own_starts = jnp.sum(jnp.where(before, own_sizes[None, :], 0), axis=1)
    slot_offset = lax.broadcasted_iota(jnp.int32, (ng, cap), 1)
    frame_slot = own_starts[:, None] + slot_offset
    slot_live = slot_offset < own_sizes[:, None]
    frame_iota = lax.broadcasted_iota(jnp.int32, (ng, cap, n_frames), 2)
    sender = (
        ((frame_iota == frame_slot[:, :, None]) & slot_live[:, :, None])
        .astype(bf16)
        .reshape(slots, n_frames)
    )
    in_sizes = pick_entry(clip_len[0], grp_index, 1)
    arrive_at = pick_entry(first_token[0], grp_index, 1)
    token_iota = lax.broadcasted_iota(jnp.int32, (toks, ng, cap), 0)
    receive_mask = (token_iota == (arrive_at[:, None] + slot_offset)[None]) & (
        slot_offset < in_sizes[:, None]
    )[None]
    receiver = receive_mask.astype(bf16).reshape(toks, slots)
    is_audio = jnp.any(receive_mask, axis=(1, 2))

    doc_iota = lax.broadcasted_iota(jnp.int32, (toks, keep.shape[0]), 1)
    kept = jnp.sum(jnp.where(segment[:, None] == doc_iota, keep[None, :], 0), axis=1)
    grad_tok = cotangent * kept.astype(bf16)[:, None]
    grad_slots = exchange(dot(receiver, grad_tok, 0, 0).astype(bf16).reshape(ng, cap, cols), GRP)
    grad_frames = dot(sender, grad_slots.reshape(slots, cols), 0, 0).astype(bf16)
    grad_text = jnp.where(is_audio[:, None], jnp.zeros_like(grad_tok), grad_tok)
    grad_rows = jnp.concatenate([grad_text, grad_frames], axis=0)

    piece = width // (ny * nx)
    w_piece = lax.dynamic_index_in_dim(frozen.reshape(2, ny, nx, piece, cols), x_index, 2, False)
    down_half = lax.dynamic_slice_in_dim(down.T, lax.rem(tp_index, 2) * width, width, 1)
    down_half = jnp.moveaxis(down_half.reshape(rank, nt, cols), 1, 0).reshape(nt * rank, cols)

    def for_y(k):
        w = lax.dynamic_index_in_dim(w_piece, lax.rem(y_index + k, ny), 1, False)
        return jnp.concatenate([w.reshape(2 * piece, cols), down_half], axis=0)

    y_parts = [for_y(0)] + [
        lax.ppermute(for_y(k), "y", [(i, (i + k) % ny) for i in range(ny)]) for k in range(1, ny)
    ]
    y_parts = jnp.stack([lax.select_n(lax.rem(y_index - j + ny, ny), *y_parts) for j in range(ny)])
    wa = y_parts[:, : 2 * piece].reshape(nt, piece, cols)
    down_t = lax.dynamic_index_in_dim(y_parts[:, 2 * piece :], tp_index // 2, 0, False)
    down_t = jnp.moveaxis(down_t.reshape(nt, rank, cols), 0, 1).reshape(rank, width)
    up_rows = rank // nx
    up_piece = lax.dynamic_slice_in_dim(up, x_index * up_rows, up_rows, 0)
    sent = jnp.concatenate(
        [wa, copies(jnp.concatenate([up_piece, grad_frames], axis=0), nt)], axis=1
    )
    text_wide = text.astype(f32)
    text_scaled = text_wide * gain[None, :]
    pair = jnp.concatenate(
        [
            (adapter_scale * dot(grad_text, up, 1, 1)).astype(bf16),
            dot(text_scaled.astype(bf16), down_t, 1, 1).astype(bf16),
        ],
        axis=1,
    )
    pair = lax.psum_scatter(pair, TP, scatter_dimension=0, tiled=True)
    sq_text = dot(jnp.ones((8, width), bf16), (text_wide * text_wide).astype(bf16), 1, 1)[0]

    came = exchange(sent, TP)
    at = piece + up_rows

    grad_full = jnp.moveaxis(came[:, at:], 0, 1).reshape(n_frames, nt * cols)
    grad_all = jnp.concatenate(from_peers(grad_full, "y"), axis=0)
    weights = jnp.moveaxis(came[:, :at], 0, 1).reshape(at, nt * cols)
    weights = lax.all_gather(weights, "x")
    up_full = weights[:, piece:].reshape(rank, nt * cols)
    weights = weights[:, :piece].reshape(nx * piece, nt * cols)
    lora_frames = (adapter_scale * dot(grad_full, up_full, 1, 1)).astype(bf16)
    spread = dot(grad_all, weights, 1, 1).astype(bf16).reshape(ny, n_frames, nx * piece)
    back = jnp.moveaxis(exchange(in_order(spread, "y"), "y"), 0, 1)
    grad_norm = back.reshape(n_frames, width).astype(f32)
    grad_norm = grad_norm + dot(lora_frames, down_t, 1, 0)
    weights = lax.all_gather(weights, "y", axis=0, tiled=True)

    blocks = exchange(x_sum.reshape(nzl, n_frames, width), "zl")
    embedded = jnp.sum(blocks.astype(f32), axis=0).astype(bf16)
    wide = embedded.astype(f32)
    scaled = wide * gain[None, :]

    sq_hi, sq_lo = two_halves(jnp.sum(wide * wide, axis=1, keepdims=True))
    d_hi, d_lo = two_halves(jnp.sum(scaled * grad_norm, axis=1, keepdims=True))
    low_frames = dot(scaled.astype(bf16), down_t, 1, 1).astype(bf16)
    spare = jnp.zeros((n_frames, cols - rank - 4), bf16)
    of_frames = jnp.concatenate([low_frames, sq_hi, sq_lo, d_hi, d_lo, spare], axis=1)
    n_l = toks // cols
    t_hi, t_lo = two_halves(sq_text.reshape(n_l, cols))
    spare = jnp.zeros((8 - 2 * n_l, cols), bf16)
    stats = jnp.concatenate([of_frames, t_hi, t_lo, spare, pair], axis=0)
    stats = exchange(copies(stats, nt), TP)
    pair = stats[:, n_frames + 8 :].reshape(toks, cols)
    stats = jnp.sum(stats[:, : n_frames + 8].astype(f32), axis=0)
    sq_frames = stats[:n_frames, rank : rank + 1] + stats[:n_frames, rank + 1 : rank + 2]
    dots = stats[:n_frames, rank + 2 : rank + 3] + stats[:n_frames, rank + 3 : rank + 4]
    sq_text = (stats[n_frames : n_frames + n_l] + stats[n_frames + n_l : n_frames + 2 * n_l]).reshape(toks, 1)
    inv_rms = lax.rsqrt(jnp.concatenate([sq_text, sq_frames], axis=0) / full_width + norm_eps)
    lora = jnp.concatenate([pair[:, :rank], lora_frames], axis=0)
    low = jnp.concatenate([pair[:, rank:].astype(f32), stats[:n_frames, :rank]], axis=0)
    low_half = (low * inv_rms).astype(bf16)

    all_scaled = jnp.concatenate([text_scaled, scaled], axis=0)
    base = dot(all_scaled.astype(bf16), weights, 1, 0).astype(bf16)
    base = jnp.moveaxis(base.reshape(rows, nt, cols), 1, 0).reshape(nt * rows, cols)
    summed = lax.psum_scatter(base, TP, scatter_dimension=0, tiled=True)
    values = summed.astype(f32) * inv_rms + adapter_scale * dot(low_half, up, 1, 0)
    values = values.astype(bf16)

    normed = (all_scaled * inv_rms).astype(bf16)
    k = rank // ng
    down_part = dot(lora, normed, 0, 0).astype(bf16).reshape(nzl, nx, k, width)
    up_part = (adapter_scale * dot(low_half, grad_rows, 0, 0)).astype(bf16)
    up_part = jnp.pad(up_part, ((0, 0), (0, width - cols))).reshape(nzl, nx, k, width)
    adapters = jnp.concatenate([down_part, up_part], axis=2).reshape(nzl, nx * 2 * k, width)

    inv_f = after(inv_rms[toks:], base)
    frame_grad = (
        inv_f * gain[None, :] * grad_norm - wide * (inv_f * inv_f * inv_f * dots / full_width)
    ).astype(bf16)
    near = to_peers(
        lambda z: jnp.concatenate([frame_grad, lax.dynamic_index_in_dim(adapters, z, 0, False)], axis=0), "zl"
    )
    adapters = sum(b[n_frames:].astype(f32) for b in near).astype(bf16).reshape(nx, 2 * k, width)
    frame_grad = placed([b[:n_frames] for b in near], 0, "zl")
    came = exchange(jnp.concatenate([copies(frame_grad, nx), adapters], axis=1), "x")
    adapters = jnp.sum(came[:, nzl * n_frames :].astype(f32), axis=0).astype(bf16)
    all_grad = came[:, : nzl * n_frames].reshape(nx, nzl, n_frames, width)
    all_grad = jnp.moveaxis(all_grad, 0, 1).reshape(ng * n_frames, width)
    proj_part = after(dot(frames, all_grad, 0, 0), summed).astype(bf16)
    part = frames.shape[1] // ny
    came = exchange(
        jnp.concatenate([proj_part.reshape(ny, part, width), copies(adapters, ny)], axis=1), "y"
    )
    came = jnp.sum(came.astype(f32), axis=0)
    projector_grad = lax.all_gather(came[:part].astype(bf16), "y", axis=0, tiled=True).astype(f32)

    n_d = k * width // cols
    own = jnp.concatenate([came[part : part + k].reshape(n_d, cols), came[part + k :, :cols]], axis=0)
    out_slots = dot(sender, values[toks:], 1, 0).reshape(ng, cap, cols)
    last = exchange(jnp.concatenate([copies(own, ng), out_slots], axis=1), GRP)
    down_grad = last[:, :n_d].reshape(rank, width).T
    up_grad = last[:, n_d : n_d + k].reshape(rank, cols)
    in_slots = last[:, n_d + k :].astype(bf16).reshape(slots, cols)
    audio_values = dot(receiver, in_slots, 1, 0).astype(bf16)
    value_output = jnp.where(is_audio[:, None], audio_values, values[:toks])
    return value_output, projector_grad, down_grad, up_grad


def solution(mesh):
    sizes = dict(zip(mesh.axis_names, mesh.devices.shape))
    half = sizes["grp"] // 4
    mesh = Mesh(
        mesh.devices.reshape(half, 4, sizes["fsdp"], sizes["tp"] // 2, 2),
        ("zl", "x", "y", "zh", "c"),
    )
    rows = ("zl", "x", "y")
    in_specs = (
        P("y", GRP),
        P(GRP, TP),
        P(rows, TP),
        P(),
        P("y", TP),
        P("y", None),
        P(None, TP),
        P("y", None, None),
        P("y", None, None),
        P(rows),
        P(),
        P(rows, TP),
    )
    out_specs = (P(rows, TP), P(GRP, TP), P(TP, None), P(None, TP))
    return jax.shard_map(shards, mesh=mesh, in_specs=in_specs, out_specs=out_specs, check_vma=False)
```

```python
import jax
import jax.numpy as jnp
from jax import lax
from jax.sharding import Mesh, PartitionSpec as P

adapter_scale = 2.0
norm_eps = 1e-05
GRP = ("zl", "x")
TP = ("zh", "c")
bf16, f32 = jnp.bfloat16, jnp.float32


def dot(a, b, ca, cb):
    return lax.dot_general(a, b, (((ca,), (cb,)), ((), ())), preferred_element_type=f32)


def exchange(blocks, axis):
    return lax.all_to_all(blocks, axis, split_axis=0, concat_axis=0, tiled=True)


def pick_entry(grid_in, position, which_axis):
    matches = lax.broadcasted_iota(jnp.int32, grid_in.shape, which_axis) == position
    return jnp.sum(jnp.where(matches, grid_in, 0), axis=which_axis)


def after(x, other):
    return x + (other[(0,) * other.ndim] * 0).astype(x.dtype)


def copies(x, n):
    return jnp.broadcast_to(x[None], (n, *x.shape))


def two_halves(v):
    hi = lax.reduce_precision(v, 8, 7)
    return hi.astype(bf16), (v - hi).astype(bf16)


def to_peers(blocks, axis):
    n, me = lax.axis_size(axis), lax.axis_index(axis)
    return [blocks(me)] + [
        lax.ppermute(blocks(lax.rem(me + k, n)), axis, [(i, (i + k) % n) for i in range(n)])
        for k in range(1, n)
    ]


def placed(blocks, dim, axis):
    n, me, size = len(blocks), lax.axis_index(axis), blocks[0].shape[dim]
    shape = list(blocks[0].shape)
    shape[dim] *= n
    out = jnp.zeros(shape, blocks[0].dtype)
    for k, block in enumerate(blocks):
        out = lax.dynamic_update_slice_in_dim(out, block, lax.rem(me - k + n, n) * size, dim)
    return out


def shards(
    frames,
    projector,
    text,
    gain_all,
    frozen,
    down,
    up,
    clip_len,
    first_token,
    segment,
    keep,
    cotangent,
):
    nx, ny, nzl, ng, nt = (lax.axis_size(a) for a in ("x", "y", "zl", GRP, TP))
    grp_index, tp_index = lax.axis_index(GRP), lax.axis_index(TP)
    x_index, y_index = lax.axis_index("x"), lax.axis_index("y")
    toks, width = text.shape
    cols, rank = frozen.shape[1], down.shape[1]
    n_frames = frames.shape[0] // ng
    full_width = width * nt
    cap = 2 * n_frames // ng
    slots = ng * cap
    rows = toks + n_frames
    gain = lax.dynamic_slice_in_dim(gain_all, tp_index * width, width, 0)

    by_x = jnp.moveaxis(frames.reshape(nzl, nx, n_frames, frames.shape[1]), 1, 0)
    partial = dot(by_x.reshape(frames.shape), projector, 1, 0).astype(bf16)
    x_sum = lax.psum_scatter(partial, "x", scatter_dimension=0, tiled=True)

    own_sizes = pick_entry(clip_len[0], grp_index, 0)
    before = lax.broadcasted_iota(jnp.int32, (ng, ng), 1) < lax.broadcasted_iota(jnp.int32, (ng, ng), 0)
    own_starts = jnp.sum(jnp.where(before, own_sizes[None, :], 0), axis=1)
    slot_offset = lax.broadcasted_iota(jnp.int32, (ng, cap), 1)
    frame_slot = own_starts[:, None] + slot_offset
    slot_live = slot_offset < own_sizes[:, None]
    frame_iota = lax.broadcasted_iota(jnp.int32, (ng, cap, n_frames), 2)
    sender = (
        ((frame_iota == frame_slot[:, :, None]) & slot_live[:, :, None])
        .astype(bf16)
        .reshape(slots, n_frames)
    )
    in_sizes = pick_entry(clip_len[0], grp_index, 1)
    arrive_at = pick_entry(first_token[0], grp_index, 1)
    token_iota = lax.broadcasted_iota(jnp.int32, (toks, ng, cap), 0)
    receive_mask = (token_iota == (arrive_at[:, None] + slot_offset)[None]) & (
        slot_offset < in_sizes[:, None]
    )[None]
    receiver = receive_mask.astype(bf16).reshape(toks, slots)
    is_audio = jnp.any(receive_mask, axis=(1, 2))

    doc_iota = lax.broadcasted_iota(jnp.int32, (toks, keep.shape[0]), 1)
    kept = jnp.sum(jnp.where(segment[:, None] == doc_iota, keep[None, :], 0), axis=1)
    grad_tok = cotangent * kept.astype(bf16)[:, None]
    grad_slots = exchange(dot(receiver, grad_tok, 0, 0).astype(bf16).reshape(ng, cap, cols), GRP)
    grad_frames = dot(sender, grad_slots.reshape(slots, cols), 0, 0).astype(bf16)
    grad_text = jnp.where(is_audio[:, None], jnp.zeros_like(grad_tok), grad_tok)
    grad_rows = jnp.concatenate([grad_text, grad_frames], axis=0)

    piece = width // (ny * nx)
    w_piece = lax.dynamic_index_in_dim(frozen.reshape(2, ny, nx, piece, cols), x_index, 2, False)
    down_half = lax.dynamic_slice_in_dim(down.T, lax.rem(tp_index, 2) * width, width, 1)
    down_half = jnp.moveaxis(down_half.reshape(rank, nt, cols), 1, 0).reshape(nt * rank, cols)

    def for_y(k):
        w = lax.dynamic_index_in_dim(w_piece, lax.rem(y_index + k, ny), 1, False)
        return jnp.concatenate([w.reshape(2 * piece, cols), down_half], axis=0)

    y_parts = [for_y(0)] + [
        lax.ppermute(for_y(k), "y", [(i, (i + k) % ny) for i in range(ny)]) for k in range(1, ny)
    ]
    y_parts = jnp.stack([lax.select_n(lax.rem(y_index - j + ny, ny), *y_parts) for j in range(ny)])
    wa = y_parts[:, : 2 * piece].reshape(nt, piece, cols)
    down_t = lax.dynamic_index_in_dim(y_parts[:, 2 * piece :], tp_index // 2, 0, False)
    down_t = jnp.moveaxis(down_t.reshape(nt, rank, cols), 0, 1).reshape(rank, width)
    up_rows = rank // nx
    up_piece = lax.dynamic_slice_in_dim(up, x_index * up_rows, up_rows, 0)
    text_wide = text.astype(f32)
    text_scaled = text_wide * gain[None, :]
    pair = jnp.concatenate(
        [
            (adapter_scale * dot(grad_text, up, 1, 1)).astype(bf16),
            dot(text_scaled.astype(bf16), down_t, 1, 1).astype(bf16),
        ],
        axis=1,
    )
    sq_text = dot(jnp.ones((8, width), bf16), (text_wide * text_wide).astype(bf16), 1, 1)[0]

    sent = jnp.concatenate(
        [
            wa,
            copies(jnp.concatenate([up_piece, grad_frames], axis=0), nt),
            pair.reshape(nt, toks // nt, cols),
        ],
        axis=1,
    )
    came = exchange(sent, TP)
    at = piece + up_rows
    pair = jnp.sum(came[:, at + n_frames :].astype(f32), axis=0).astype(bf16)

    blocks = exchange(x_sum.reshape(nzl, n_frames, width), "zl")
    embedded = jnp.sum(blocks.astype(f32), axis=0).astype(bf16)
    wide = embedded.astype(f32)
    scaled = wide * gain[None, :]

    grad_full = jnp.moveaxis(came[:, at : at + n_frames], 0, 1).reshape(n_frames, nt * cols)
    grad_all = lax.all_gather(grad_full, "y", axis=0, tiled=True)
    weights = jnp.moveaxis(came[:, :at], 0, 1).reshape(at, nt * cols)
    weights = lax.all_gather(weights, "x")
    up_full = weights[:, piece:].reshape(rank, nt * cols)
    weights = weights[:, :piece].reshape(nx * piece, nt * cols)
    lora_frames = (adapter_scale * dot(grad_full, up_full, 1, 1)).astype(bf16)
    spread = dot(grad_all, weights, 1, 1).astype(bf16).reshape(ny, n_frames, nx * piece)
    back = jnp.moveaxis(exchange(after(spread, embedded), "y"), 0, 1)
    grad_norm = back.reshape(n_frames, width).astype(f32)
    grad_norm = grad_norm + dot(lora_frames, down_t, 1, 0)
    weights = lax.all_gather(weights, "y", axis=0, tiled=True)

    sq_hi, sq_lo = two_halves(jnp.sum(wide * wide, axis=1, keepdims=True))
    d_hi, d_lo = two_halves(jnp.sum(scaled * grad_norm, axis=1, keepdims=True))
    low_frames = dot(scaled.astype(bf16), down_t, 1, 1).astype(bf16)
    spare = jnp.zeros((n_frames, cols - rank - 4), bf16)
    of_frames = jnp.concatenate([low_frames, sq_hi, sq_lo, d_hi, d_lo, spare], axis=1)
    n_l = toks // cols
    t_hi, t_lo = two_halves(sq_text.reshape(n_l, cols))
    spare = jnp.zeros((8 - 2 * n_l, cols), bf16)
    stats = jnp.concatenate([of_frames, t_hi, t_lo, spare, pair], axis=0)
    stats = exchange(copies(stats, nt), TP)
    pair = stats[:, n_frames + 8 :].reshape(toks, cols)
    stats = jnp.sum(stats[:, : n_frames + 8].astype(f32), axis=0)
    sq_frames = stats[:n_frames, rank : rank + 1] + stats[:n_frames, rank + 1 : rank + 2]
    dots = stats[:n_frames, rank + 2 : rank + 3] + stats[:n_frames, rank + 3 : rank + 4]
    sq_text = (stats[n_frames : n_frames + n_l] + stats[n_frames + n_l : n_frames + 2 * n_l]).reshape(toks, 1)
    inv_rms = lax.rsqrt(jnp.concatenate([sq_text, sq_frames], axis=0) / full_width + norm_eps)
    lora = jnp.concatenate([pair[:, :rank], lora_frames], axis=0)
    low = jnp.concatenate([pair[:, rank:].astype(f32), stats[:n_frames, :rank]], axis=0)
    low_half = (low * inv_rms).astype(bf16)

    all_scaled = jnp.concatenate([text_scaled, scaled], axis=0)
    base = dot(all_scaled.astype(bf16), weights, 1, 0).astype(bf16)
    base = jnp.moveaxis(base.reshape(rows, nt, cols), 1, 0).reshape(nt * rows, cols)
    summed = lax.psum_scatter(base, TP, scatter_dimension=0, tiled=True)
    values = summed.astype(f32) * inv_rms + adapter_scale * dot(low_half, up, 1, 0)
    values = values.astype(bf16)

    normed = (all_scaled * inv_rms).astype(bf16)
    k = rank // ng
    down_part = dot(lora, normed, 0, 0).astype(bf16).reshape(nzl, nx, k, width)
    up_part = (adapter_scale * dot(low_half, grad_rows, 0, 0)).astype(bf16)
    up_part = jnp.pad(up_part, ((0, 0), (0, width - cols))).reshape(nzl, nx, k, width)
    adapters = jnp.concatenate([down_part, up_part], axis=2).reshape(nzl, nx * 2 * k, width)

    inv_f = after(inv_rms[toks:], base)
    frame_grad = (
        inv_f * gain[None, :] * grad_norm - wide * (inv_f * inv_f * inv_f * dots / full_width)
    ).astype(bf16)
    near = to_peers(
        lambda z: jnp.concatenate([frame_grad, lax.dynamic_index_in_dim(adapters, z, 0, False)], axis=0), "zl"
    )
    adapters = sum(b[n_frames:].astype(f32) for b in near).astype(bf16).reshape(nx, 2 * k, width)
    frame_grad = placed([b[:n_frames] for b in near], 0, "zl")
    came = exchange(jnp.concatenate([copies(frame_grad, nx), adapters], axis=1), "x")
    adapters = jnp.sum(came[:, nzl * n_frames :].astype(f32), axis=0).astype(bf16)
    all_grad = came[:, : nzl * n_frames].reshape(nx, nzl, n_frames, width)
    all_grad = jnp.moveaxis(all_grad, 0, 1).reshape(ng * n_frames, width)
    proj_part = after(dot(frames, all_grad, 0, 0), summed).astype(bf16)
    part = frames.shape[1] // ny
    came = exchange(
        jnp.concatenate([proj_part.reshape(ny, part, width), copies(adapters, ny)], axis=1), "y"
    )
    came = jnp.sum(came.astype(f32), axis=0)
    projector_grad = lax.all_gather(came[:part].astype(bf16), "y", axis=0, tiled=True).astype(f32)

    n_d = k * width // cols
    own = jnp.concatenate([came[part : part + k].reshape(n_d, cols), came[part + k :, :cols]], axis=0)
    out_slots = dot(sender, values[toks:], 1, 0).reshape(ng, cap, cols)
    last = exchange(jnp.concatenate([copies(own, ng), out_slots], axis=1), GRP)
    down_grad = last[:, :n_d].reshape(rank, width).T
    up_grad = last[:, n_d : n_d + k].reshape(rank, cols)
    in_slots = last[:, n_d + k :].astype(bf16).reshape(slots, cols)
    audio_values = dot(receiver, in_slots, 1, 0).astype(bf16)
    value_output = jnp.where(is_audio[:, None], audio_values, values[:toks])
    return value_output, projector_grad, down_grad, up_grad


def solution(mesh):
    sizes = dict(zip(mesh.axis_names, mesh.devices.shape))
    half = sizes["grp"] // 4
    mesh = Mesh(
        mesh.devices.reshape(half, 4, sizes["fsdp"], sizes["tp"] // 2, 2),
        ("zl", "x", "y", "zh", "c"),
    )
    rows = ("zl", "x", "y")
    in_specs = (
        P("y", GRP),
        P(GRP, TP),
        P(rows, TP),
        P(),
        P("y", TP),
        P("y", None),
        P(None, TP),
        P("y", None, None),
        P("y", None, None),
        P(rows),
        P(),
        P(rows, TP),
    )
    out_specs = (P(rows, TP), P(GRP, TP), P(TP, None), P(None, TP))
    return jax.shard_map(shards, mesh=mesh, in_specs=in_specs, out_specs=out_specs, check_vma=False)
```

```python
import jax
import jax.numpy as jnp
from jax import lax
from jax.sharding import Mesh, PartitionSpec as P

adapter_scale = 2.0
norm_eps = 1e-05
GRP = ("zl", "x")
TP = ("zh", "c")
bf16, f32 = jnp.bfloat16, jnp.float32


def dot(a, b, ca, cb):
    return lax.dot_general(a, b, (((ca,), (cb,)), ((), ())), preferred_element_type=f32)


def exchange(blocks, axis):
    return lax.all_to_all(blocks, axis, split_axis=0, concat_axis=0, tiled=True)


def pick_entry(grid_in, position, which_axis):
    matches = lax.broadcasted_iota(jnp.int32, grid_in.shape, which_axis) == position
    return jnp.sum(jnp.where(matches, grid_in, 0), axis=which_axis)


def after(x, other):
    return x + (other[(0,) * other.ndim] * 0).astype(x.dtype)


def copies(x, n):
    return jnp.broadcast_to(x[None], (n, *x.shape))


def two_halves(v):
    hi = lax.reduce_precision(v, 8, 7)
    return hi.astype(bf16), (v - hi).astype(bf16)


def to_peers(blocks, axis):
    n, me = lax.axis_size(axis), lax.axis_index(axis)
    return [blocks(me)] + [
        lax.ppermute(blocks(lax.rem(me + k, n)), axis, [(i, (i + k) % n) for i in range(n)])
        for k in range(1, n)
    ]


def placed(blocks, dim, axis):
    n, me, size = len(blocks), lax.axis_index(axis), blocks[0].shape[dim]
    shape = list(blocks[0].shape)
    shape[dim] *= n
    out = jnp.zeros(shape, blocks[0].dtype)
    for k, block in enumerate(blocks):
        out = lax.dynamic_update_slice_in_dim(out, block, lax.rem(me - k + n, n) * size, dim)
    return out


def shards(
    frames,
    projector,
    text,
    gain_all,
    frozen,
    down,
    up,
    clip_len,
    first_token,
    segment,
    keep,
    cotangent,
):
    nx, ny, nzl, ng, nt = (lax.axis_size(a) for a in ("x", "y", "zl", GRP, TP))
    grp_index, tp_index = lax.axis_index(GRP), lax.axis_index(TP)
    x_index, y_index = lax.axis_index("x"), lax.axis_index("y")
    toks, width = text.shape
    cols, rank = frozen.shape[1], down.shape[1]
    n_frames = frames.shape[0] // ng
    full_width = width * nt
    cap = 2 * n_frames // ng
    slots = ng * cap
    rows = toks + n_frames
    gain = lax.dynamic_slice_in_dim(gain_all, tp_index * width, width, 0)

    by_x = jnp.moveaxis(frames.reshape(nzl, nx, n_frames, frames.shape[1]), 1, 0)
    partial = dot(by_x.reshape(frames.shape), projector, 1, 0).astype(bf16)
    x_sum = lax.psum_scatter(partial, "x", scatter_dimension=0, tiled=True)
    all_frames = lax.all_gather(by_x.reshape(frames.shape), "y", axis=0, tiled=True)

    own_sizes = pick_entry(clip_len[0], grp_index, 0)
    before = lax.broadcasted_iota(jnp.int32, (ng, ng), 1) < lax.broadcasted_iota(jnp.int32, (ng, ng), 0)
    own_starts = jnp.sum(jnp.where(before, own_sizes[None, :], 0), axis=1)
    slot_offset = lax.broadcasted_iota(jnp.int32, (ng, cap), 1)
    frame_slot = own_starts[:, None] + slot_offset
    slot_live = slot_offset < own_sizes[:, None]
    frame_iota = lax.broadcasted_iota(jnp.int32, (ng, cap, n_frames), 2)
    sender = (
        ((frame_iota == frame_slot[:, :, None]) & slot_live[:, :, None])
        .astype(bf16)
        .reshape(slots, n_frames)
    )
    in_sizes = pick_entry(clip_len[0], grp_index, 1)
    arrive_at = pick_entry(first_token[0], grp_index, 1)
    token_iota = lax.broadcasted_iota(jnp.int32, (toks, ng, cap), 0)
    receive_mask = (token_iota == (arrive_at[:, None] + slot_offset)[None]) & (
        slot_offset < in_sizes[:, None]
    )[None]
    receiver = receive_mask.astype(bf16).reshape(toks, slots)
    is_audio = jnp.any(receive_mask, axis=(1, 2))

    doc_iota = lax.broadcasted_iota(jnp.int32, (toks, keep.shape[0]), 1)
    kept = jnp.sum(jnp.where(segment[:, None] == doc_iota, keep[None, :], 0), axis=1)
    grad_tok = cotangent * kept.astype(bf16)[:, None]
    grad_slots = exchange(dot(receiver, grad_tok, 0, 0).astype(bf16).reshape(ng, cap, cols), GRP)
    grad_frames = dot(sender, grad_slots.reshape(slots, cols), 0, 0).astype(bf16)
    grad_text = jnp.where(is_audio[:, None], jnp.zeros_like(grad_tok), grad_tok)
    grad_rows = jnp.concatenate([grad_text, grad_frames], axis=0)

    piece = width // (ny * nx)
    w_piece = lax.dynamic_index_in_dim(frozen.reshape(2, ny, nx, piece, cols), x_index, 2, False)
    down_half = lax.dynamic_slice_in_dim(down.T, lax.rem(tp_index, 2) * width, width, 1)
    down_half = jnp.moveaxis(down_half.reshape(rank, nt, cols), 1, 0).reshape(nt * rank, cols)

    def for_y(k):
        w = lax.dynamic_index_in_dim(w_piece, lax.rem(y_index + k, ny), 1, False)
        return jnp.concatenate([w.reshape(2 * piece, cols), down_half], axis=0)

    y_parts = [for_y(0)] + [
        lax.ppermute(for_y(k), "y", [(i, (i + k) % ny) for i in range(ny)]) for k in range(1, ny)
    ]
    y_parts = jnp.stack([lax.select_n(lax.rem(y_index - j + ny, ny), *y_parts) for j in range(ny)])
    wa = y_parts[:, : 2 * piece].reshape(nt, piece, cols)
    down_t = lax.dynamic_index_in_dim(y_parts[:, 2 * piece :], tp_index // 2, 0, False)
    down_t = jnp.moveaxis(down_t.reshape(nt, rank, cols), 0, 1).reshape(rank, width)
    up_rows = rank // nx
    up_piece = lax.dynamic_slice_in_dim(up, x_index * up_rows, up_rows, 0)
    text_wide = text.astype(f32)
    text_scaled = text_wide * gain[None, :]
    pair = jnp.concatenate(
        [
            (adapter_scale * dot(grad_text, up, 1, 1)).astype(bf16),
            dot(text_scaled.astype(bf16), down_t, 1, 1).astype(bf16),
        ],
        axis=1,
    )
    sq_text = dot(jnp.ones((8, width), bf16), (text_wide * text_wide).astype(bf16), 1, 1)[0]

    sent = jnp.concatenate(
        [
            wa,
            copies(jnp.concatenate([up_piece, grad_frames], axis=0), nt),
            pair.reshape(nt, toks // nt, cols),
        ],
        axis=1,
    )
    came = exchange(sent, TP)
    at = piece + up_rows
    pair = jnp.sum(came[:, at + n_frames :].astype(f32), axis=0).astype(bf16)

    blocks = exchange(x_sum.reshape(nzl, n_frames, width), "zl")
    embedded = jnp.sum(blocks.astype(f32), axis=0).astype(bf16)
    wide = embedded.astype(f32)
    scaled = wide * gain[None, :]

    grad_full = jnp.moveaxis(came[:, at : at + n_frames], 0, 1).reshape(n_frames, nt * cols)
    grad_all = lax.all_gather(after(grad_full, all_frames), "y", axis=0, tiled=True)
    weights = jnp.moveaxis(came[:, :at], 0, 1).reshape(at, nt * cols)
    weights = lax.all_gather(weights, "x")
    up_full = weights[:, piece:].reshape(rank, nt * cols)
    weights = weights[:, :piece].reshape(nx * piece, nt * cols)
    lora_frames = (adapter_scale * dot(grad_full, up_full, 1, 1)).astype(bf16)
    spread = dot(grad_all, weights, 1, 1).astype(bf16).reshape(ny, n_frames, nx * piece)
    back = jnp.moveaxis(exchange(after(spread, embedded), "y"), 0, 1)
    grad_norm = back.reshape(n_frames, width).astype(f32)
    grad_norm = grad_norm + dot(lora_frames, down_t, 1, 0)
    weights = lax.all_gather(weights, "y", axis=0, tiled=True)

    sq_hi, sq_lo = two_halves(jnp.sum(wide * wide, axis=1, keepdims=True))
    d_hi, d_lo = two_halves(jnp.sum(scaled * grad_norm, axis=1, keepdims=True))
    low_frames = dot(scaled.astype(bf16), down_t, 1, 1).astype(bf16)
    spare = jnp.zeros((n_frames, cols - rank - 4), bf16)
    of_frames = jnp.concatenate([low_frames, sq_hi, sq_lo, d_hi, d_lo, spare], axis=1)
    n_l = toks // cols
    t_hi, t_lo = two_halves(sq_text.reshape(n_l, cols))
    spare = jnp.zeros((8 - 2 * n_l, cols), bf16)
    stats = jnp.concatenate([of_frames, t_hi, t_lo, spare, pair], axis=0)
    stats = exchange(copies(stats, nt), TP)
    pair = stats[:, n_frames + 8 :].reshape(toks, cols)
    stats = jnp.sum(stats[:, : n_frames + 8].astype(f32), axis=0)
    sq_frames = stats[:n_frames, rank : rank + 1] + stats[:n_frames, rank + 1 : rank + 2]
    dots = stats[:n_frames, rank + 2 : rank + 3] + stats[:n_frames, rank + 3 : rank + 4]
    sq_text = (stats[n_frames : n_frames + n_l] + stats[n_frames + n_l : n_frames + 2 * n_l]).reshape(toks, 1)
    inv_rms = lax.rsqrt(jnp.concatenate([sq_text, sq_frames], axis=0) / full_width + norm_eps)
    lora = jnp.concatenate([pair[:, :rank], lora_frames], axis=0)
    low = jnp.concatenate([pair[:, rank:].astype(f32), stats[:n_frames, :rank]], axis=0)
    low_half = (low * inv_rms).astype(bf16)

    all_scaled = jnp.concatenate([text_scaled, scaled], axis=0)
    base = dot(all_scaled.astype(bf16), weights, 1, 0).astype(bf16)
    base = jnp.moveaxis(base.reshape(rows, nt, cols), 1, 0).reshape(nt * rows, cols)
    summed = lax.psum_scatter(base, TP, scatter_dimension=0, tiled=True)

    normed = (all_scaled * inv_rms).astype(bf16)
    quarter = width // ny
    down_part = dot(lora, normed, 0, 0).astype(bf16).reshape(nzl, ny * nx, width)
    up_part = (adapter_scale * dot(low_half, grad_rows, 0, 0)).astype(bf16)
    up_part = jnp.pad(up_part, ((0, 0), (0, width - cols))).reshape(nzl, ny * nx, width)
    adapters = jnp.concatenate([down_part, up_part], axis=1)

    inv_f = after(inv_rms[toks:], base)
    frame_grad = (
        inv_f * gain[None, :] * grad_norm - wide * (inv_f * inv_f * inv_f * dots / full_width)
    ).astype(bf16)
    near = to_peers(
        lambda z: jnp.concatenate([frame_grad, lax.dynamic_index_in_dim(adapters, z, 0, False)], axis=0), "zl"
    )
    adapters = sum(b[n_frames:].astype(f32) for b in near).astype(bf16)
    frame_grad = placed([b[:n_frames] for b in near], 0, "zl")

    n_x = nzl * n_frames
    frame_grad = jnp.moveaxis(frame_grad.reshape(n_x, ny, quarter), 1, 0)
    frame_grad = jnp.broadcast_to(frame_grad[:, None], (ny, nx, n_x, quarter))
    frame_grad = frame_grad.reshape(ny * nx, n_x, quarter)
    down_part = adapters[: ny * nx].reshape(ny * nx, ny, quarter)
    up_part = adapters[ny * nx :, :quarter].reshape(ny * nx, 1, quarter)
    spare = jnp.zeros((ny * nx, 7 - ny, quarter), bf16)
    came = exchange(jnp.concatenate([frame_grad, down_part, up_part, spare], axis=1), ("y", "x"))
    own = jnp.sum(came[:, n_x : n_x + ny + 1].astype(f32), axis=0).astype(bf16)
    own = jnp.concatenate([own[:ny].reshape(width // cols, cols), own[ny:, :cols]], axis=0)

    values = summed.astype(f32) * inv_rms + adapter_scale * dot(low_half, up, 1, 0)
    values = values.astype(bf16)
    out_slots = dot(sender, values[toks:], 1, 0).astype(bf16).reshape(nzl, 1, nx, cap, cols)
    out_slots = jnp.broadcast_to(out_slots, (nzl, ny, nx, cap, cols)).reshape(ny * ng, cap, cols)
    last = exchange(jnp.concatenate([copies(own, ny * ng), out_slots], axis=1), ("zl", "y", "x"))
    n_d = width // cols
    down_grad = last[:, :n_d].reshape(rank, width).astype(f32).T
    up_grad = last[:, n_d].astype(f32)
    all_grad = came[:, :n_x].reshape(ny * nx * n_x, quarter)
    projector_grad = after(dot(all_frames, all_grad, 0, 0), summed).astype(bf16)
    projector_grad = lax.all_gather(projector_grad, "y", axis=1, tiled=True).astype(f32)

    in_slots = last[:, -cap:].reshape(nzl, ny, nx * cap, cols)
    in_slots = lax.dynamic_index_in_dim(in_slots, y_index, 1, False).reshape(slots, cols)
    audio_values = dot(receiver, in_slots, 1, 0).astype(bf16)
    value_output = jnp.where(is_audio[:, None], audio_values, values[:toks])
    return value_output, projector_grad, down_grad, up_grad


def solution(mesh):
    sizes = dict(zip(mesh.axis_names, mesh.devices.shape))
    half = sizes["grp"] // 4
    mesh = Mesh(
        mesh.devices.reshape(half, 4, sizes["fsdp"], sizes["tp"] // 2, 2),
        ("zl", "x", "y", "zh", "c"),
    )
    rows = ("zl", "x", "y")
    in_specs = (
        P("y", GRP),
        P(GRP, TP),
        P(rows, TP),
        P(),
        P("y", TP),
        P("y", None),
        P(None, TP),
        P("y", None, None),
        P("y", None, None),
        P(rows),
        P(),
        P(rows, TP),
    )
    out_specs = (P(rows, TP), P(GRP, TP), P(TP, None), P(None, TP))
    return jax.shard_map(shards, mesh=mesh, in_specs=in_specs, out_specs=out_specs, check_vma=False)
```

```python
import jax
import jax.numpy as jnp
from jax import lax
from jax.sharding import Mesh, PartitionSpec as P

adapter_scale = 2.0
norm_eps = 1e-05
GRP = ("zl", "x")
TP = ("zh", "c")
bf16, f32 = jnp.bfloat16, jnp.float32


def dot(a, b, ca, cb):
    return lax.dot_general(a, b, (((ca,), (cb,)), ((), ())), preferred_element_type=f32)


def exchange(blocks, axis):
    return lax.all_to_all(blocks, axis, split_axis=0, concat_axis=0, tiled=True)


def pick_entry(grid_in, position, which_axis):
    matches = lax.broadcasted_iota(jnp.int32, grid_in.shape, which_axis) == position
    return jnp.sum(jnp.where(matches, grid_in, 0), axis=which_axis)


def after(x, other):
    return x + (other[(0,) * other.ndim] * 0).astype(x.dtype)


def copies(x, n):
    return jnp.broadcast_to(x[None], (n, *x.shape))


def two_halves(v):
    hi = lax.reduce_precision(v, 8, 7)
    return hi.astype(bf16), (v - hi).astype(bf16)


def to_peers(blocks, axis):
    n, me = lax.axis_size(axis), lax.axis_index(axis)
    return [blocks(me)] + [
        lax.ppermute(blocks(lax.rem(me + k, n)), axis, [(i, (i + k) % n) for i in range(n)])
        for k in range(1, n)
    ]


def placed(blocks, dim, axis):
    n, me, size = len(blocks), lax.axis_index(axis), blocks[0].shape[dim]
    shape = list(blocks[0].shape)
    shape[dim] *= n
    out = jnp.zeros(shape, blocks[0].dtype)
    for k, block in enumerate(blocks):
        out = lax.dynamic_update_slice_in_dim(out, block, lax.rem(me - k + n, n) * size, dim)
    return out


def shards(
    frames,
    projector,
    text,
    gain_all,
    frozen,
    down,
    up,
    clip_len,
    first_token,
    segment,
    keep,
    cotangent,
):
    nx, ny, nzl, ng, nt = (lax.axis_size(a) for a in ("x", "y", "zl", GRP, TP))
    grp_index, tp_index = lax.axis_index(GRP), lax.axis_index(TP)
    x_index, y_index = lax.axis_index("x"), lax.axis_index("y")
    toks, width = text.shape
    cols, rank = frozen.shape[1], down.shape[1]
    n_frames = frames.shape[0] // ng
    full_width = width * nt
    cap = 2 * n_frames // ng
    slots = ng * cap
    rows = toks + n_frames
    gain = lax.dynamic_slice_in_dim(gain_all, tp_index * width, width, 0)

    by_x = jnp.moveaxis(frames.reshape(nzl, nx, n_frames, frames.shape[1]), 1, 0)
    partial = dot(by_x.reshape(frames.shape), projector, 1, 0).astype(bf16)
    x_sum = lax.psum_scatter(partial, "x", scatter_dimension=0, tiled=True)
    all_frames = lax.all_gather(by_x.reshape(frames.shape), "y", axis=0, tiled=True)

    own_sizes = pick_entry(clip_len[0], grp_index, 0)
    before = lax.broadcasted_iota(jnp.int32, (ng, ng), 1) < lax.broadcasted_iota(jnp.int32, (ng, ng), 0)
    own_starts = jnp.sum(jnp.where(before, own_sizes[None, :], 0), axis=1)
    slot_offset = lax.broadcasted_iota(jnp.int32, (ng, cap), 1)
    frame_slot = own_starts[:, None] + slot_offset
    slot_live = slot_offset < own_sizes[:, None]
    frame_iota = lax.broadcasted_iota(jnp.int32, (ng, cap, n_frames), 2)
    sender = (
        ((frame_iota == frame_slot[:, :, None]) & slot_live[:, :, None])
        .astype(bf16)
        .reshape(slots, n_frames)
    )
    in_sizes = pick_entry(clip_len[0], grp_index, 1)
    arrive_at = pick_entry(first_token[0], grp_index, 1)
    token_iota = lax.broadcasted_iota(jnp.int32, (toks, ng, cap), 0)
    receive_mask = (token_iota == (arrive_at[:, None] + slot_offset)[None]) & (
        slot_offset < in_sizes[:, None]
    )[None]
    receiver = receive_mask.astype(bf16).reshape(toks, slots)
    is_audio = jnp.any(receive_mask, axis=(1, 2))

    doc_iota = lax.broadcasted_iota(jnp.int32, (toks, keep.shape[0]), 1)
    kept = jnp.sum(jnp.where(segment[:, None] == doc_iota, keep[None, :], 0), axis=1)
    grad_tok = cotangent * kept.astype(bf16)[:, None]
    grad_slots = exchange(dot(receiver, grad_tok, 0, 0).astype(bf16).reshape(ng, cap, cols), GRP)
    grad_frames = dot(sender, grad_slots.reshape(slots, cols), 0, 0).astype(bf16)
    grad_text = jnp.where(is_audio[:, None], jnp.zeros_like(grad_tok), grad_tok)
    grad_rows = jnp.concatenate([grad_text, grad_frames], axis=0)

    piece = width // (ny * nx)
    w_piece = lax.dynamic_index_in_dim(frozen.reshape(2, ny, nx, piece, cols), x_index, 2, False)
    down_half = lax.dynamic_slice_in_dim(down.T, lax.rem(tp_index, 2) * width, width, 1)
    down_half = jnp.moveaxis(down_half.reshape(rank, nt, cols), 1, 0).reshape(nt * rank, cols)

    def for_y(k):
        w = lax.dynamic_index_in_dim(w_piece, lax.rem(y_index + k, ny), 1, False)
        return jnp.concatenate([w.reshape(2 * piece, cols), down_half], axis=0)

    y_parts = [for_y(0)] + [
        lax.ppermute(for_y(k), "y", [(i, (i + k) % ny) for i in range(ny)]) for k in range(1, ny)
    ]
    y_parts = jnp.stack([lax.select_n(lax.rem(y_index - j + ny, ny), *y_parts) for j in range(ny)])
    wa = y_parts[:, : 2 * piece].reshape(nt, piece, cols)
    down_t = lax.dynamic_index_in_dim(y_parts[:, 2 * piece :], tp_index // 2, 0, False)
    down_t = jnp.moveaxis(down_t.reshape(nt, rank, cols), 0, 1).reshape(rank, width)
    up_rows = rank // nx
    up_piece = lax.dynamic_slice_in_dim(up, x_index * up_rows, up_rows, 0)
    text_wide = text.astype(f32)
    text_scaled = text_wide * gain[None, :]
    pair = jnp.concatenate(
        [
            (adapter_scale * dot(grad_text, up, 1, 1)).astype(bf16),
            dot(text_scaled.astype(bf16), down_t, 1, 1).astype(bf16),
        ],
        axis=1,
    )
    sq_text = dot(jnp.ones((8, width), bf16), (text_wide * text_wide).astype(bf16), 1, 1)[0]

    sent = jnp.concatenate(
        [
            wa,
            copies(jnp.concatenate([up_piece, grad_frames], axis=0), nt),
            pair.reshape(nt, toks // nt, cols),
        ],
        axis=1,
    )
    came = exchange(sent, TP)
    at = piece + up_rows
    pair = jnp.sum(came[:, at + n_frames :].astype(f32), axis=0).astype(bf16)

    blocks = exchange(x_sum.reshape(nzl, n_frames, width), "zl")
    embedded = jnp.sum(blocks.astype(f32), axis=0).astype(bf16)
    wide = embedded.astype(f32)
    scaled = wide * gain[None, :]

    grad_full = jnp.moveaxis(came[:, at : at + n_frames], 0, 1).reshape(n_frames, nt * cols)
    grad_all = lax.all_gather(grad_full, "y", axis=0, tiled=True)
    weights = jnp.moveaxis(came[:, :at], 0, 1).reshape(at, nt * cols)
    weights = lax.all_gather(weights, "x")
    up_full = weights[:, piece:].reshape(rank, nt * cols)
    weights = weights[:, :piece].reshape(nx * piece, nt * cols)
    lora_frames = (adapter_scale * dot(grad_full, up_full, 1, 1)).astype(bf16)
    spread = dot(grad_all, weights, 1, 1).astype(bf16).reshape(ny, n_frames, nx * piece)
    back = jnp.moveaxis(exchange(after(spread, embedded), "y"), 0, 1)
    grad_norm = back.reshape(n_frames, width).astype(f32)
    grad_norm = grad_norm + dot(lora_frames, down_t, 1, 0)
    weights = lax.all_gather(weights, "y", axis=0, tiled=True)

    sq_hi, sq_lo = two_halves(jnp.sum(wide * wide, axis=1, keepdims=True))
    d_hi, d_lo = two_halves(jnp.sum(scaled * grad_norm, axis=1, keepdims=True))
    low_frames = dot(scaled.astype(bf16), down_t, 1, 1).astype(bf16)
    spare = jnp.zeros((n_frames, cols - rank - 4), bf16)
    of_frames = jnp.concatenate([low_frames, sq_hi, sq_lo, d_hi, d_lo, spare], axis=1)
    n_l = toks // cols
    t_hi, t_lo = two_halves(sq_text.reshape(n_l, cols))
    spare = jnp.zeros((8 - 2 * n_l, cols), bf16)
    stats = jnp.concatenate([of_frames, t_hi, t_lo, spare, pair], axis=0)
    stats = exchange(copies(stats, nt), TP)
    pair = stats[:, n_frames + 8 :].reshape(toks, cols)
    stats = jnp.sum(stats[:, : n_frames + 8].astype(f32), axis=0)
    sq_frames = stats[:n_frames, rank : rank + 1] + stats[:n_frames, rank + 1 : rank + 2]
    dots = stats[:n_frames, rank + 2 : rank + 3] + stats[:n_frames, rank + 3 : rank + 4]
    sq_text = (stats[n_frames : n_frames + n_l] + stats[n_frames + n_l : n_frames + 2 * n_l]).reshape(toks, 1)
    inv_rms = lax.rsqrt(jnp.concatenate([sq_text, sq_frames], axis=0) / full_width + norm_eps)
    lora = jnp.concatenate([pair[:, :rank], lora_frames], axis=0)
    low = jnp.concatenate([pair[:, rank:].astype(f32), stats[:n_frames, :rank]], axis=0)
    low_half = (low * inv_rms).astype(bf16)

    all_scaled = jnp.concatenate([text_scaled, scaled], axis=0)
    base = dot(all_scaled.astype(bf16), weights, 1, 0).astype(bf16)
    base = jnp.moveaxis(base.reshape(rows, nt, cols), 1, 0).reshape(nt * rows, cols)
    summed = lax.psum_scatter(base, TP, scatter_dimension=0, tiled=True)

    normed = (all_scaled * inv_rms).astype(bf16)
    quarter = width // ny
    down_part = dot(lora, normed, 0, 0).astype(bf16).reshape(nzl, ny * nx, width)
    up_part = (adapter_scale * dot(low_half, grad_rows, 0, 0)).astype(bf16)
    up_part = jnp.pad(up_part, ((0, 0), (0, width - cols))).reshape(nzl, ny * nx, width)
    adapters = jnp.concatenate([down_part, up_part], axis=1)

    inv_f = after(inv_rms[toks:], base)
    frame_grad = (
        inv_f * gain[None, :] * grad_norm - wide * (inv_f * inv_f * inv_f * dots / full_width)
    ).astype(bf16)
    near = to_peers(
        lambda z: jnp.concatenate([frame_grad, lax.dynamic_index_in_dim(adapters, z, 0, False)], axis=0), "zl"
    )
    adapters = sum(b[n_frames:].astype(f32) for b in near).astype(bf16)
    frame_grad = placed([b[:n_frames] for b in near], 0, "zl")

    n_x = nzl * n_frames
    frame_grad = jnp.moveaxis(frame_grad.reshape(n_x, ny, quarter), 1, 0)
    frame_grad = jnp.broadcast_to(frame_grad[:, None], (ny, nx, n_x, quarter))
    frame_grad = frame_grad.reshape(ny * nx, n_x, quarter)
    down_part = adapters[: ny * nx].reshape(ny * nx, ny, quarter)
    up_part = adapters[ny * nx :, :quarter].reshape(ny * nx, 1, quarter)
    spare = jnp.zeros((ny * nx, 7 - ny, quarter), bf16)
    came = exchange(jnp.concatenate([frame_grad, down_part, up_part, spare], axis=1), ("y", "x"))
    own = jnp.sum(came[:, n_x : n_x + ny + 1].astype(f32), axis=0).astype(bf16)
    own = jnp.concatenate([own[:ny].reshape(width // cols, cols), own[ny:, :cols]], axis=0)

    values = summed.astype(f32) * inv_rms + adapter_scale * dot(low_half, up, 1, 0)
    values = values.astype(bf16)
    out_slots = dot(sender, values[toks:], 1, 0).astype(bf16).reshape(nzl, 1, nx, cap, cols)
    out_slots = jnp.broadcast_to(out_slots, (nzl, ny, nx, cap, cols)).reshape(ny * ng, cap, cols)
    last = exchange(jnp.concatenate([copies(own, ny * ng), out_slots], axis=1), ("zl", "y", "x"))
    n_d = width // cols
    down_grad = last[:, :n_d].reshape(rank, width).astype(f32).T
    up_grad = last[:, n_d].astype(f32)
    all_grad = came[:, :n_x].reshape(ny * nx * n_x, quarter)
    projector_grad = after(dot(all_frames, all_grad, 0, 0), summed).astype(bf16)
    projector_grad = lax.all_gather(projector_grad, "y", axis=1, tiled=True).astype(f32)

    in_slots = last[:, -cap:].reshape(nzl, ny, nx * cap, cols)
    in_slots = lax.dynamic_index_in_dim(in_slots, y_index, 1, False).reshape(slots, cols)
    audio_values = dot(receiver, in_slots, 1, 0).astype(bf16)
    value_output = jnp.where(is_audio[:, None], audio_values, values[:toks])
    return value_output, projector_grad, down_grad, up_grad


def solution(mesh):
    sizes = dict(zip(mesh.axis_names, mesh.devices.shape))
    half = sizes["grp"] // 4
    mesh = Mesh(
        mesh.devices.reshape(half, 4, sizes["fsdp"], sizes["tp"] // 2, 2),
        ("zl", "x", "y", "zh", "c"),
    )
    rows = ("zl", "x", "y")
    in_specs = (
        P("y", GRP),
        P(GRP, TP),
        P(rows, TP),
        P(),
        P("y", TP),
        P("y", None),
        P(None, TP),
        P("y", None, None),
        P("y", None, None),
        P(rows),
        P(),
        P(rows, TP),
    )
    out_specs = (P(rows, TP), P(GRP, TP), P(TP, None), P(None, TP))
    return jax.shard_map(shards, mesh=mesh, in_specs=in_specs, out_specs=out_specs, check_vma=False)
```

```python
import jax
import jax.numpy as jnp
from jax import lax
from jax.sharding import Mesh, PartitionSpec as P

adapter_scale = 2.0
norm_eps = 1e-05
GRP = ("zl", "x")
TP = ("zh", "c")
bf16, f32 = jnp.bfloat16, jnp.float32


def dot(a, b, ca, cb):
    return lax.dot_general(a, b, (((ca,), (cb,)), ((), ())), preferred_element_type=f32)


def exchange(blocks, axis):
    return lax.all_to_all(blocks, axis, split_axis=0, concat_axis=0, tiled=True)


def pick_entry(grid_in, position, which_axis):
    matches = lax.broadcasted_iota(jnp.int32, grid_in.shape, which_axis) == position
    return jnp.sum(jnp.where(matches, grid_in, 0), axis=which_axis)


def after(x, other):
    return x + (other[(0,) * other.ndim] * 0).astype(x.dtype)


def copies(x, n):
    return jnp.broadcast_to(x[None], (n, *x.shape))


def two_halves(v):
    hi = lax.reduce_precision(v, 8, 7)
    return hi.astype(bf16), (v - hi).astype(bf16)


def shards(
    frames,
    projector,
    text,
    gain_all,
    frozen,
    down,
    up,
    clip_len,
    first_token,
    segment,
    keep,
    cotangent,
):
    nx, ny, nzl, ng, nt = (lax.axis_size(a) for a in ("x", "y", "zl", GRP, TP))
    grp_index, tp_index = lax.axis_index(GRP), lax.axis_index(TP)
    x_index, y_index = lax.axis_index("x"), lax.axis_index("y")
    toks, width = text.shape
    cols, rank = frozen.shape[1], down.shape[1]
    n_frames = frames.shape[0] // ng
    full_width = width * nt
    cap = 2 * n_frames // ng
    slots = ng * cap
    rows = toks + n_frames
    gain = lax.dynamic_slice_in_dim(gain_all, tp_index * width, width, 0)

    by_x = jnp.moveaxis(frames.reshape(nzl, nx, n_frames, frames.shape[1]), 1, 0)
    partial = dot(by_x.reshape(frames.shape), projector, 1, 0).astype(bf16)
    x_sum = lax.psum_scatter(partial, "x", scatter_dimension=0, tiled=True)
    all_frames = lax.all_gather(by_x.reshape(frames.shape), "y", axis=0, tiled=True)

    own_sizes = pick_entry(clip_len[0], grp_index, 0)
    before = lax.broadcasted_iota(jnp.int32, (ng, ng), 1) < lax.broadcasted_iota(jnp.int32, (ng, ng), 0)
    own_starts = jnp.sum(jnp.where(before, own_sizes[None, :], 0), axis=1)
    slot_offset = lax.broadcasted_iota(jnp.int32, (ng, cap), 1)
    frame_slot = own_starts[:, None] + slot_offset
    slot_live = slot_offset < own_sizes[:, None]
    frame_iota = lax.broadcasted_iota(jnp.int32, (ng, cap, n_frames), 2)
    sender = (
        ((frame_iota == frame_slot[:, :, None]) & slot_live[:, :, None])
        .astype(bf16)
        .reshape(slots, n_frames)
    )
    in_sizes = pick_entry(clip_len[0], grp_index, 1)
    arrive_at = pick_entry(first_token[0], grp_index, 1)
    token_iota = lax.broadcasted_iota(jnp.int32, (toks, ng, cap), 0)
    receive_mask = (token_iota == (arrive_at[:, None] + slot_offset)[None]) & (
        slot_offset < in_sizes[:, None]
    )[None]
    receiver = receive_mask.astype(bf16).reshape(toks, slots)
    is_audio = jnp.any(receive_mask, axis=(1, 2))

    doc_iota = lax.broadcasted_iota(jnp.int32, (toks, keep.shape[0]), 1)
    kept = jnp.sum(jnp.where(segment[:, None] == doc_iota, keep[None, :], 0), axis=1)
    grad_tok = cotangent * kept.astype(bf16)[:, None]
    grad_slots = exchange(dot(receiver, grad_tok, 0, 0).astype(bf16).reshape(ng, cap, cols), GRP)
    grad_frames = dot(sender, grad_slots.reshape(slots, cols), 0, 0).astype(bf16)
    grad_text = jnp.where(is_audio[:, None], jnp.zeros_like(grad_tok), grad_tok)
    grad_rows = jnp.concatenate([grad_text, grad_frames], axis=0)

    piece = width // (ny * nx)
    w_piece = lax.dynamic_index_in_dim(frozen.reshape(2, ny, nx, piece, cols), x_index, 2, False)
    down_half = lax.dynamic_slice_in_dim(down.T, lax.rem(tp_index, 2) * width, width, 1)
    down_half = jnp.moveaxis(down_half.reshape(rank, nt, cols), 1, 0).reshape(nt * rank, cols)

    def for_y(k):
        w = lax.dynamic_index_in_dim(w_piece, lax.rem(y_index + k, ny), 1, False)
        return jnp.concatenate([w.reshape(2 * piece, cols), down_half], axis=0)

    y_parts = [for_y(0)] + [
        lax.ppermute(for_y(k), "y", [(i, (i + k) % ny) for i in range(ny)]) for k in range(1, ny)
    ]
    y_parts = jnp.stack([lax.select_n(lax.rem(y_index - j + ny, ny), *y_parts) for j in range(ny)])
    wa = y_parts[:, : 2 * piece].reshape(nt, piece, cols)
    down_t = lax.dynamic_index_in_dim(y_parts[:, 2 * piece :], tp_index // 2, 0, False)
    down_t = jnp.moveaxis(down_t.reshape(nt, rank, cols), 0, 1).reshape(rank, width)
    up_rows = rank // nx
    up_piece = lax.dynamic_slice_in_dim(up, x_index * up_rows, up_rows, 0)
    text_wide = text.astype(f32)
    text_scaled = text_wide * gain[None, :]
    pair = jnp.concatenate(
        [
            (adapter_scale * dot(grad_text, up, 1, 1)).astype(bf16),
            dot(text_scaled.astype(bf16), down_t, 1, 1).astype(bf16),
        ],
        axis=1,
    )
    sq_text = dot(jnp.ones((8, width), bf16), (text_wide * text_wide).astype(bf16), 1, 1)[0]

    sent = jnp.concatenate(
        [
            wa,
            copies(jnp.concatenate([up_piece, grad_frames], axis=0), nt),
            pair.reshape(nt, toks // nt, cols),
        ],
        axis=1,
    )
    came = exchange(sent, TP)
    at = piece + up_rows
    pair = jnp.sum(came[:, at + n_frames :].astype(f32), axis=0).astype(bf16)

    blocks = exchange(x_sum.reshape(nzl, n_frames, width), "zl")
    embedded = jnp.sum(blocks.astype(f32), axis=0).astype(bf16)
    wide = embedded.astype(f32)
    scaled = wide * gain[None, :]

    grad_full = jnp.moveaxis(came[:, at : at + n_frames], 0, 1).reshape(n_frames, nt * cols)
    grad_all = lax.all_gather(grad_full, "y", axis=0, tiled=True)
    weights = jnp.moveaxis(came[:, :at], 0, 1).reshape(at, nt * cols)
    weights = lax.all_gather(weights, "x")
    up_full = weights[:, piece:].reshape(rank, nt * cols)
    weights = weights[:, :piece].reshape(nx * piece, nt * cols)
    lora_frames = (adapter_scale * dot(grad_full, up_full, 1, 1)).astype(bf16)
    spread = dot(grad_all, weights, 1, 1).astype(bf16).reshape(ny, n_frames, nx * piece)
    back = jnp.moveaxis(exchange(after(spread, embedded), "y"), 0, 1)
    grad_norm = back.reshape(n_frames, width).astype(f32)
    grad_norm = grad_norm + dot(lora_frames, down_t, 1, 0)
    weights = lax.all_gather(weights, "y", axis=0, tiled=True)

    sq_hi, sq_lo = two_halves(jnp.sum(wide * wide, axis=1, keepdims=True))
    d_hi, d_lo = two_halves(jnp.sum(scaled * grad_norm, axis=1, keepdims=True))
    low_frames = dot(scaled.astype(bf16), down_t, 1, 1).astype(bf16)
    spare = jnp.zeros((n_frames, cols - rank - 4), bf16)
    of_frames = jnp.concatenate([low_frames, sq_hi, sq_lo, d_hi, d_lo, spare], axis=1)
    n_l = toks // cols
    t_hi, t_lo = two_halves(sq_text.reshape(n_l, cols))
    spare = jnp.zeros((8 - 2 * n_l, cols), bf16)
    stats = jnp.concatenate([of_frames, t_hi, t_lo, spare, pair], axis=0)
    stats = exchange(copies(stats, nt), TP)
    pair = stats[:, n_frames + 8 :].reshape(toks, cols)
    stats = jnp.sum(stats[:, : n_frames + 8].astype(f32), axis=0)
    sq_frames = stats[:n_frames, rank : rank + 1] + stats[:n_frames, rank + 1 : rank + 2]
    dots = stats[:n_frames, rank + 2 : rank + 3] + stats[:n_frames, rank + 3 : rank + 4]
    sq_text = (stats[n_frames : n_frames + n_l] + stats[n_frames + n_l : n_frames + 2 * n_l]).reshape(toks, 1)
    inv_rms = lax.rsqrt(jnp.concatenate([sq_text, sq_frames], axis=0) / full_width + norm_eps)
    lora = jnp.concatenate([pair[:, :rank], lora_frames], axis=0)
    low = jnp.concatenate([pair[:, rank:].astype(f32), stats[:n_frames, :rank]], axis=0)
    low_half = (low * inv_rms).astype(bf16)

    all_scaled = jnp.concatenate([text_scaled, scaled], axis=0)
    base = dot(all_scaled.astype(bf16), weights, 1, 0).astype(bf16)
    base = jnp.moveaxis(base.reshape(rows, nt, cols), 1, 0).reshape(nt * rows, cols)
    summed = lax.psum_scatter(base, TP, scatter_dimension=0, tiled=True)

    normed = (all_scaled * inv_rms).astype(bf16)
    quarter = width // ny
    down_part = dot(lora, normed, 0, 0).astype(bf16).reshape(nzl, ny * nx, width)
    up_part = (adapter_scale * dot(low_half, grad_rows, 0, 0)).astype(bf16)
    up_part = jnp.pad(up_part, ((0, 0), (0, width - cols))).reshape(nzl, ny * nx, width)
    adapters = jnp.concatenate([down_part, up_part], axis=1)

    inv_f = after(inv_rms[toks:], base)
    frame_grad = (
        inv_f * gain[None, :] * grad_norm - wide * (inv_f * inv_f * inv_f * dots / full_width)
    ).astype(bf16)
    came = exchange(jnp.concatenate([copies(frame_grad, nzl), adapters], axis=1), "zl")
    adapters = jnp.sum(came[:, n_frames:].astype(f32), axis=0).astype(bf16)
    frame_grad = came[:, :n_frames]

    n_x = nzl * n_frames
    frame_grad = jnp.moveaxis(frame_grad.reshape(n_x, ny, quarter), 1, 0)
    frame_grad = jnp.broadcast_to(frame_grad[:, None], (ny, nx, n_x, quarter))
    frame_grad = frame_grad.reshape(ny * nx, n_x, quarter)
    down_part = adapters[: ny * nx].reshape(ny * nx, ny, quarter)
    up_part = adapters[ny * nx :, :quarter].reshape(ny * nx, 1, quarter)
    spare = jnp.zeros((ny * nx, 7 - ny, quarter), bf16)
    came = exchange(jnp.concatenate([frame_grad, down_part, up_part, spare], axis=1), ("y", "x"))
    own = jnp.sum(came[:, n_x : n_x + ny + 1].astype(f32), axis=0).astype(bf16)
    own = jnp.concatenate([own[:ny].reshape(width // cols, cols), own[ny:, :cols]], axis=0)

    values = summed.astype(f32) * inv_rms + adapter_scale * dot(low_half, up, 1, 0)
    values = values.astype(bf16)
    out_slots = dot(sender, values[toks:], 1, 0).astype(bf16).reshape(nzl, 1, nx, cap, cols)
    out_slots = jnp.broadcast_to(out_slots, (nzl, ny, nx, cap, cols)).reshape(ny * ng, cap, cols)
    last = exchange(jnp.concatenate([copies(own, ny * ng), out_slots], axis=1), ("zl", "y", "x"))
    n_d = width // cols
    down_grad = last[:, :n_d].reshape(rank, width).astype(f32).T
    up_grad = last[:, n_d].astype(f32)
    all_grad = came[:, :n_x].reshape(ny * nx * n_x, quarter)
    projector_grad = after(dot(all_frames, all_grad, 0, 0), summed).astype(bf16)
    projector_grad = lax.all_gather(projector_grad, "y", axis=1, tiled=True).astype(f32)

    in_slots = last[:, -cap:].reshape(nzl, ny, nx * cap, cols)
    in_slots = lax.dynamic_index_in_dim(in_slots, y_index, 1, False).reshape(slots, cols)
    audio_values = dot(receiver, in_slots, 1, 0).astype(bf16)
    value_output = jnp.where(is_audio[:, None], audio_values, values[:toks])
    return value_output, projector_grad, down_grad, up_grad


def solution(mesh):
    sizes = dict(zip(mesh.axis_names, mesh.devices.shape))
    half = sizes["grp"] // 4
    mesh = Mesh(
        mesh.devices.reshape(half, 4, sizes["fsdp"], sizes["tp"] // 2, 2),
        ("zl", "x", "y", "zh", "c"),
    )
    rows = ("zl", "x", "y")
    in_specs = (
        P("y", GRP),
        P(GRP, TP),
        P(rows, TP),
        P(),
        P("y", TP),
        P("y", None),
        P(None, TP),
        P("y", None, None),
        P("y", None, None),
        P(rows),
        P(),
        P(rows, TP),
    )
    out_specs = (P(rows, TP), P(GRP, TP), P(TP, None), P(None, TP))
    return jax.shard_map(shards, mesh=mesh, in_specs=in_specs, out_specs=out_specs, check_vma=False)
```

```python
import jax
import jax.numpy as jnp
from jax import lax
from jax.sharding import Mesh, PartitionSpec as P

adapter_scale = 2.0
norm_eps = 1e-05
GRP = ("zl", "x")
TP = ("zh", "c")
bf16, f32 = jnp.bfloat16, jnp.float32


def dot(a, b, ca, cb):
    return lax.dot_general(a, b, (((ca,), (cb,)), ((), ())), preferred_element_type=f32)


def exchange(blocks, axis):
    return lax.all_to_all(blocks, axis, split_axis=0, concat_axis=0, tiled=True)


def pick_entry(grid_in, position, which_axis):
    matches = lax.broadcasted_iota(jnp.int32, grid_in.shape, which_axis) == position
    return jnp.sum(jnp.where(matches, grid_in, 0), axis=which_axis)


def after(x, other):
    return x + (other[(0,) * other.ndim] * 0).astype(x.dtype)


def copies(x, n):
    return jnp.broadcast_to(x[None], (n, *x.shape))


def two_halves(v):
    hi = lax.reduce_precision(v, 8, 7)
    return hi.astype(bf16), (v - hi).astype(bf16)


def shards(
    frames,
    projector,
    text,
    gain_all,
    frozen,
    down,
    up,
    clip_len,
    first_token,
    segment,
    keep,
    cotangent,
):
    nx, ny, nzl, ng, nt = (lax.axis_size(a) for a in ("x", "y", "zl", GRP, TP))
    grp_index, tp_index = lax.axis_index(GRP), lax.axis_index(TP)
    x_index, y_index = lax.axis_index("x"), lax.axis_index("y")
    toks, width = text.shape
    cols, rank = frozen.shape[1], down.shape[1]
    n_frames = frames.shape[0] // ng
    full_width = width * nt
    cap = 2 * n_frames // ng
    slots = ng * cap
    rows = toks + n_frames
    gain = lax.dynamic_slice_in_dim(gain_all, tp_index * width, width, 0)

    by_x = jnp.moveaxis(frames.reshape(nzl, nx, n_frames, frames.shape[1]), 1, 0)
    partial = dot(by_x.reshape(frames.shape), projector, 1, 0).astype(bf16)
    x_sum = lax.psum_scatter(partial, "x", scatter_dimension=0, tiled=True)
    all_frames = jnp.pad(by_x.reshape(nx, nzl * n_frames, -1), ((0, 0), (0, 8), (0, 0)))
    all_frames = lax.all_gather(all_frames.reshape(nx * (nzl * n_frames + 8), -1), "y", axis=0, tiled=True)

    own_sizes = pick_entry(clip_len[0], grp_index, 0)
    before = lax.broadcasted_iota(jnp.int32, (ng, ng), 1) < lax.broadcasted_iota(jnp.int32, (ng, ng), 0)
    own_starts = jnp.sum(jnp.where(before, own_sizes[None, :], 0), axis=1)
    slot_offset = lax.broadcasted_iota(jnp.int32, (ng, cap), 1)
    frame_slot = own_starts[:, None] + slot_offset
    slot_live = slot_offset < own_sizes[:, None]
    frame_iota = lax.broadcasted_iota(jnp.int32, (ng, cap, n_frames), 2)
    sender = (
        ((frame_iota == frame_slot[:, :, None]) & slot_live[:, :, None])
        .astype(bf16)
        .reshape(slots, n_frames)
    )
    in_sizes = pick_entry(clip_len[0], grp_index, 1)
    arrive_at = pick_entry(first_token[0], grp_index, 1)
    token_iota = lax.broadcasted_iota(jnp.int32, (toks, ng, cap), 0)
    receive_mask = (token_iota == (arrive_at[:, None] + slot_offset)[None]) & (
        slot_offset < in_sizes[:, None]
    )[None]
    receiver = receive_mask.astype(bf16).reshape(toks, slots)
    is_audio = jnp.any(receive_mask, axis=(1, 2))

    doc_iota = lax.broadcasted_iota(jnp.int32, (toks, keep.shape[0]), 1)
    kept = jnp.sum(jnp.where(segment[:, None] == doc_iota, keep[None, :], 0), axis=1)
    grad_tok = cotangent * kept.astype(bf16)[:, None]
    grad_slots = exchange(dot(receiver, grad_tok, 0, 0).astype(bf16).reshape(ng, cap, cols), GRP)
    grad_frames = dot(sender, grad_slots.reshape(slots, cols), 0, 0).astype(bf16)
    grad_text = jnp.where(is_audio[:, None], jnp.zeros_like(grad_tok), grad_tok)
    grad_rows = jnp.concatenate([grad_text, grad_frames], axis=0)

    piece = width // (ny * nx)
    w_piece = lax.dynamic_index_in_dim(frozen.reshape(2, ny, nx, piece, cols), x_index, 2, False)
    down_half = lax.dynamic_slice_in_dim(down.T, lax.rem(tp_index, 2) * width, width, 1)
    down_half = jnp.moveaxis(down_half.reshape(rank, nt, cols), 1, 0).reshape(nt * rank, cols)

    def for_y(k):
        w = lax.dynamic_index_in_dim(w_piece, lax.rem(y_index + k, ny), 1, False)
        return jnp.concatenate([w.reshape(2 * piece, cols), down_half], axis=0)

    y_parts = [for_y(0)] + [
        lax.ppermute(for_y(k), "y", [(i, (i + k) % ny) for i in range(ny)]) for k in range(1, ny)
    ]
    y_parts = jnp.stack([lax.select_n(lax.rem(y_index - j + ny, ny), *y_parts) for j in range(ny)])
    wa = y_parts[:, : 2 * piece].reshape(nt, piece, cols)
    down_t = lax.dynamic_index_in_dim(y_parts[:, 2 * piece :], tp_index // 2, 0, False)
    down_t = jnp.moveaxis(down_t.reshape(nt, rank, cols), 0, 1).reshape(rank, width)
    up_rows = rank // nx
    up_piece = lax.dynamic_slice_in_dim(up, x_index * up_rows, up_rows, 0)
    text_wide = text.astype(f32)
    text_scaled = text_wide * gain[None, :]
    pair = jnp.concatenate(
        [
            (adapter_scale * dot(grad_text, up, 1, 1)).astype(bf16),
            dot(text_scaled.astype(bf16), down_t, 1, 1).astype(bf16),
        ],
        axis=1,
    )
    sq_text = dot(jnp.ones((8, width), bf16), (text_wide * text_wide).astype(bf16), 1, 1)[0]

    sent = jnp.concatenate(
        [
            wa,
            copies(jnp.concatenate([up_piece, grad_frames], axis=0), nt),
            pair.reshape(nt, toks // nt, cols),
        ],
        axis=1,
    )
    came = exchange(sent, TP)
    at = piece + up_rows
    pair = jnp.sum(came[:, at + n_frames :].astype(f32), axis=0).astype(bf16)

    blocks = exchange(x_sum.reshape(nzl, n_frames, width), "zl")
    embedded = jnp.sum(blocks.astype(f32), axis=0).astype(bf16)
    wide = embedded.astype(f32)
    scaled = wide * gain[None, :]

    grad_full = jnp.moveaxis(came[:, at : at + n_frames], 0, 1).reshape(n_frames, nt * cols)
    grad_all = lax.all_gather(grad_full, "y", axis=0, tiled=True)
    weights = jnp.moveaxis(came[:, :at], 0, 1).reshape(at, nt * cols)
    weights = lax.all_gather(weights, "x")
    up_full = weights[:, piece:].reshape(rank, nt * cols)
    weights = weights[:, :piece].reshape(nx * piece, nt * cols)
    lora_frames = (adapter_scale * dot(grad_full, up_full, 1, 1)).astype(bf16)
    spread = dot(grad_all, weights, 1, 1).astype(bf16).reshape(ny, n_frames, nx * piece)
    back = jnp.moveaxis(exchange(after(spread, embedded), "y"), 0, 1)
    grad_norm = back.reshape(n_frames, width).astype(f32)
    grad_norm = grad_norm + dot(lora_frames, down_t, 1, 0)
    weights = lax.all_gather(weights, "y", axis=0, tiled=True)

    sq_hi, sq_lo = two_halves(jnp.sum(wide * wide, axis=1, keepdims=True))
    d_hi, d_lo = two_halves(jnp.sum(scaled * grad_norm, axis=1, keepdims=True))
    low_frames = dot(scaled.astype(bf16), down_t, 1, 1).astype(bf16)
    spare = jnp.zeros((n_frames, cols - rank - 4), bf16)
    of_frames = jnp.concatenate([low_frames, sq_hi, sq_lo, d_hi, d_lo, spare], axis=1)
    n_l = toks // cols
    t_hi, t_lo = two_halves(sq_text.reshape(n_l, cols))
    spare = jnp.zeros((8 - 2 * n_l, cols), bf16)
    stats = jnp.concatenate([of_frames, t_hi, t_lo, spare, pair], axis=0)
    stats = exchange(copies(stats, nt), TP)
    pair = stats[:, n_frames + 8 :].reshape(toks, cols)
    stats = jnp.sum(stats[:, : n_frames + 8].astype(f32), axis=0)
    sq_frames = stats[:n_frames, rank : rank + 1] + stats[:n_frames, rank + 1 : rank + 2]
    dots = stats[:n_frames, rank + 2 : rank + 3] + stats[:n_frames, rank + 3 : rank + 4]
    sq_text = (stats[n_frames : n_frames + n_l] + stats[n_frames + n_l : n_frames + 2 * n_l]).reshape(toks, 1)
    inv_rms = lax.rsqrt(jnp.concatenate([sq_text, sq_frames], axis=0) / full_width + norm_eps)
    lora = jnp.concatenate([pair[:, :rank], lora_frames], axis=0)
    low = jnp.concatenate([pair[:, rank:].astype(f32), stats[:n_frames, :rank]], axis=0)
    low_half = (low * inv_rms).astype(bf16)

    all_scaled = jnp.concatenate([text_scaled, scaled], axis=0)
    base = dot(all_scaled.astype(bf16), weights, 1, 0).astype(bf16)
    base = jnp.moveaxis(base.reshape(rows, nt, cols), 1, 0).reshape(nt * rows, cols)
    summed = lax.psum_scatter(base, TP, scatter_dimension=0, tiled=True)

    normed = (all_scaled * inv_rms).astype(bf16)
    quarter = width // ny
    down_part = dot(lora, normed, 0, 0).astype(bf16).reshape(nzl, ny * nx, width)
    up_part = (adapter_scale * dot(low_half, grad_rows, 0, 0)).astype(bf16)
    up_part = jnp.pad(up_part, ((0, 0), (0, width - cols))).reshape(nzl, ny * nx, width)
    adapters = jnp.concatenate([down_part, up_part], axis=1)

    inv_f = after(inv_rms[toks:], base)
    frame_grad = (
        inv_f * gain[None, :] * grad_norm - wide * (inv_f * inv_f * inv_f * dots / full_width)
    ).astype(bf16)
    came = exchange(jnp.concatenate([copies(frame_grad, nzl), adapters], axis=1), "zl")
    adapters = jnp.sum(came[:, n_frames:].astype(f32), axis=0).astype(bf16)
    frame_grad = came[:, :n_frames]

    n_x = nzl * n_frames
    frame_grad = jnp.moveaxis(frame_grad.reshape(n_x, ny, quarter), 1, 0)
    frame_grad = jnp.broadcast_to(frame_grad[:, None], (ny, nx, n_x, quarter))
    frame_grad = frame_grad.reshape(ny * nx, n_x, quarter)
    down_part = adapters[: ny * nx].reshape(ny * nx, ny, quarter)
    up_part = adapters[ny * nx :, :quarter].reshape(ny * nx, 1, quarter)
    spare = jnp.zeros((ny * nx, 7 - ny, quarter), bf16)
    came = exchange(jnp.concatenate([frame_grad, down_part, up_part, spare], axis=1), ("y", "x"))
    own = jnp.sum(came[:, n_x : n_x + ny + 1].astype(f32), axis=0).astype(bf16)
    own = jnp.concatenate([own[:ny].reshape(width // cols, cols), own[ny:, :cols]], axis=0)

    values = summed.astype(f32) * inv_rms + adapter_scale * dot(low_half, up, 1, 0)
    values = values.astype(bf16)
    out_slots = dot(sender, values[toks:], 1, 0).astype(bf16).reshape(nzl, 1, nx, cap, cols)
    out_slots = jnp.broadcast_to(out_slots, (nzl, ny, nx, cap, cols)).reshape(ny * ng, cap, cols)
    last = exchange(jnp.concatenate([copies(own, ny * ng), out_slots], axis=1), ("zl", "y", "x"))
    n_d = width // cols
    down_grad = last[:, :n_d].reshape(rank, width).astype(f32).T
    up_grad = last[:, n_d].astype(f32)
    all_grad = came.reshape(ny * nx * (n_x + 8), quarter)
    projector_grad = dot(all_frames, all_grad, 0, 0).astype(bf16)
    projector_grad = lax.all_gather(projector_grad, "y", axis=1, tiled=True).astype(f32)

    in_slots = last[:, -cap:].reshape(nzl, ny, nx * cap, cols)
    in_slots = lax.dynamic_index_in_dim(in_slots, y_index, 1, False).reshape(slots, cols)
    audio_values = dot(receiver, in_slots, 1, 0).astype(bf16)
    value_output = jnp.where(is_audio[:, None], audio_values, values[:toks])
    return value_output, projector_grad, down_grad, up_grad


def solution(mesh):
    sizes = dict(zip(mesh.axis_names, mesh.devices.shape))
    half = sizes["grp"] // 4
    mesh = Mesh(
        mesh.devices.reshape(half, 4, sizes["fsdp"], sizes["tp"] // 2, 2),
        ("zl", "x", "y", "zh", "c"),
    )
    rows = ("zl", "x", "y")
    in_specs = (
        P("y", GRP),
        P(GRP, TP),
        P(rows, TP),
        P(),
        P("y", TP),
        P("y", None),
        P(None, TP),
        P("y", None, None),
        P("y", None, None),
        P(rows),
        P(),
        P(rows, TP),
    )
    out_specs = (P(rows, TP), P(GRP, TP), P(TP, None), P(None, TP))
    return jax.shard_map(shards, mesh=mesh, in_specs=in_specs, out_specs=out_specs, check_vma=False)
```
